32 devices in a mesh: gx: 8 (over z, x), gy: 4 (over y, core).
Axes of the slice: x: 2, y: 2, z: 4, core: 2. Of those that a mesh axis runs over, the one named last changes fastest.
Arguments:
- anchors: float32 [3, 1024], P(None, ('gx', 'gy')), may hold values from 0 to 1
- directions: float32 [3, 1024], P(None, ('gx', 'gy')), may hold values from -1 to 1
- ray_start: float32 [1024], P(('gx', 'gy')), may hold values from 0 to 1
- camera_ids: int32 [1024], P(('gx', 'gy')), may hold values from 0 to 255
- brick_ids: int32 [1024, 4], P(('gx', 'gy')), may hold values from 0 to 31, all different within a row; in each aligned block of 32 rows (0 to 31, 32 to 63, ...) at most 8 rows name the same one
- brick_rank: int32 [1024, 4], P(('gx', 'gy')), may hold values from 0 to 3, each once within a row
- targets: float32 [1024, 128], P(('gx', 'gy')), may hold values from -6 to 6
- planes: float32 [32, 12288, 128], P(('gx', 'gy')), may hold values from -6 to 6
- first_weight: float32 [32, 128, 256], P(('gx', 'gy')), may hold values from -0.5 to 0.5
- hidden_weight: float32 [32, 1, 256, 256], P(('gx', 'gy')), may hold values from -0.375 to 0.375
- feature_weight: float32 [32, 256, 128], P(('gx', 'gy')), may hold values from -0.375 to 0.375
- density_weight: float32 [32, 256], P(('gx', 'gy')), may hold values from -0.375 to 0.375
- poses: float32 [6, 256], replicated, may hold values from -0.1 to 0.1
Outputs:
- ray_feature: float32 [1024, 128], P(('gx', 'gy'))
- plane_grad: float32 [32, 12288, 128], P(('gx', 'gy'))
- first_grad: float32 [32, 128, 256], P(('gx', 'gy'))
- hidden_grad: float32 [32, 1, 256, 256], P(('gx', 'gy'))
- feature_grad: float32 [32, 256, 128], P(('gx', 'gy'))
- density_grad: float32 [32, 256], P(('gx', 'gy'))
- pose_grad: float32 [6, 256], replicated
The draws below stay inside these ranges and needn't reach their ends.
Inputs may be any that keep to these rules, and one draw needn't show every extreme that they name: `brick_ids`: each ray names 4 different bricks; among the rays of one device no brick is named more than 8 times, and in every draw some device's rays name some brick exactly 8 times. `brick_rank`: each row holds every number of 0 to 3 once.
All inputs are finite; a program needn't handle non-finite values.
Results may differ from the reference program's by a relative error of at most 0.014.
Values sent between devices are 32-bit elements; how exact they have to be, the bound alone decides.
A program may use at most 256 MiB of HBM per device.

```python
import math
import jax
import jax.numpy as jnp
import numpy as np
from jax import lax

C = 128
H = 256
DEPTH = 2
K = 4
S = 4
P_SIZE = 64
NCAM = 256
RAYS_DEV = 32
BRICKS = 32
CAP = 8
RAYS = 1024


def set_ends(values, rng, least, high):
    longest = values.shape.index(max(values.shape))
    spots = []
    for shift in (0, 1):
        where = [jax.random.randint(jax.random.fold_in(rng, axis), (), 0, length) for axis, length in enumerate(values.shape)]
        where[longest] = (where[longest] + shift) % values.shape[longest]
        spots.append(tuple(where))
    return values.at[spots[0]].set(least).at[spots[1]].set(high)


def level_of(rng, dims, cuts, least, largest):
    loudness = 1.0
    for dim, blocks in cuts:
        heights = jax.random.uniform(jax.random.fold_in(jax.random.fold_in(rng, 6), dim), (blocks,), jnp.float32, least / len(cuts), largest / len(cuts))
        loudness = loudness * jnp.repeat(jnp.exp(heights), dims[dim] // blocks).reshape((-1,) + (1,) * (len(dims) - 1 - dim))
    return loudness


def shared_out(key, own, number, rows, number_of, top, bound, skew):
    order = jax.random.permutation(key, number_of)
    crowded, common = shares(number_of, rows * top, bound, skew, True), shares(number_of, rows * top, bound, skew, False)
    places = jnp.arange(number_of)

    def named(lengths, turn):
        used = int((lengths > 0).sum())
        fixed = max(1, used // 4)
        moved = fixed + (places - fixed + turn * (used - fixed)) % max(1, number_of - fixed)
        return jnp.zeros((number_of,), jnp.int32).at[order[jnp.where(places < fixed, places, moved)]].set(jnp.asarray(lengths, jnp.int32))

    lengths = jnp.where(number % 4 == 0, named(crowded, number // 4), named(common, number - number // 4 - 1))
    mixed = jax.random.permutation(jax.random.fold_in(own, 3), number_of)
    source_of, sink = mixed[0:number_of // 2 * 2:2], mixed[1:number_of // 2 * 2:2]
    slack = jnp.minimum(lengths[source_of] - 1, bound - lengths[sink]) // 2
    slack = jnp.where((source_of == order[0]) | (sink == order[0]) | (lengths[sink] == 0), 0, jnp.maximum(slack, 0))
    moved = jax.random.randint(jax.random.fold_in(own, 4), (number_of // 2,), 0, 1 << 20) % (slack + 1)
    lengths = lengths.at[source_of].add(-moved).at[sink].add(moved)
    members = jnp.searchsorted(jnp.cumsum(lengths), jnp.arange(rows * top), side="right").astype(jnp.int32)
    table = members.reshape(top, rows).T
    table = table[jax.random.permutation(jax.random.fold_in(own, 1), rows)]
    turn = jax.random.randint(jax.random.fold_in(own, 2), (rows, 1), 0, top)
    return jnp.take_along_axis(table, (jnp.arange(top)[None, :] + turn) % top, axis=1)


def shares(count, total, bound, slope, full):
    loads = [(1 << 20) // math.isqrt(grade ** slope) + 1 for grade in range(1, count + 1)]
    largest = bound if full else min(bound, max(-(-total // count), total * loads[0] // sum(loads)))
    least = 1 if total - largest >= count - 1 else 0
    counts, spare = [largest] + [least] * (count - 1), total - largest - least * (count - 1)
    while spare > 0:
        free = [i for i in range(1, count) if counts[i] < largest] or [i for i in range(1, count) if counts[i] < bound]
        mass, remaining = sum([loads[i] for i in free]), spare
        for i in free:
            addition = min(bound - counts[i], max(1, remaining * loads[i] // mass), spare)
            counts[i] = counts[i] + addition
            spare = spare - addition
    return np.array(counts)


def normal_values(own_key, shape, width, limit, split=(), kind=jnp.bfloat16):
    drawn = width * jax.random.normal(own_key, shape, jnp.float32)
    if split:
        drawn = drawn * level_of(own_key, shape, split, -0.22, 0.18)
    return jnp.clip(drawn, -limit, limit).astype(kind)


def setup_inputs(seed: int = 0) -> dict:
    key_of = jax.random.split(jax.random.key(seed), 14)
    anchors = jnp.clip(1.0 * jax.random.uniform(key_of[0], (3, RAYS), jnp.float32) ** level_of(key_of[0], (3, RAYS), ((1, 32),), -0.2, 0.2), 0.0, 1.0)
    directions = jnp.clip(jax.random.uniform(key_of[1], (3, RAYS), jnp.float32, -1.0, 1.0) * level_of(key_of[1], (3, RAYS), ((1, 32),), -0.4, 0.0), -1.0, 1.0)
    ray_start = jnp.clip(1.0 * jax.random.uniform(key_of[2], (RAYS,), jnp.float32) ** level_of(key_of[2], (RAYS,), ((0, 32),), -0.2, 0.2), 0.0, 1.0)
    camera_ids = set_ends(jax.random.randint(key_of[3], (RAYS,), 0, NCAM), jax.random.fold_in(key_of[3], 1), 0, NCAM - 1).astype(jnp.int32)
    brick_ids_keys = jax.random.split(jax.random.fold_in(key_of[4], 1), RAYS // RAYS_DEV)
    brick_ids_turns = jax.random.permutation(jax.random.fold_in(key_of[4], 3), RAYS // RAYS_DEV)
    brick_ids = jax.vmap(lambda own, number: shared_out(jax.random.fold_in(key_of[4], 2), own, number, RAYS_DEV, BRICKS, K, CAP, 2))(brick_ids_keys, brick_ids_turns).reshape((RAYS, K))
    brick_rank = jax.vmap(lambda own: jax.random.permutation(own, K))(jax.random.split(key_of[5], RAYS)).reshape((RAYS, K)).astype(jnp.int32)
    targets = normal_values(key_of[6], (RAYS, C), 1.0, 6.0, ((0, 32),), jnp.float32)
    planes = normal_values(key_of[7], (BRICKS, 3 * P_SIZE * P_SIZE, C), 1.0, 6.0, ((0, 32),), jnp.float32)
    first_weight = normal_values(key_of[8], (BRICKS, C, H), C ** -0.5, 0.5, ((0, 32),), jnp.float32)
    hidden_weight = normal_values(key_of[9], (BRICKS, DEPTH - 1, H, H), H ** -0.5, 0.375, ((0, 32),), jnp.float32)
    feature_weight = normal_values(key_of[10], (BRICKS, H, C), H ** -0.5, 0.375, ((0, 32),), jnp.float32)
    density_weight = normal_values(key_of[11], (BRICKS, H), H ** -0.5, 0.375, ((0, 32),), jnp.float32)
    poses = jnp.clip(jax.random.uniform(key_of[12], (6, NCAM), jnp.float32, -0.1, 0.1), -0.1, 0.1)
    return {"anchors": anchors, "directions": directions, "ray_start": ray_start, "camera_ids": camera_ids, "brick_ids": brick_ids, "brick_rank": brick_rank, "targets": targets, "planes": planes, "first_weight": first_weight, "hidden_weight": hidden_weight, "feature_weight": feature_weight, "density_weight": density_weight, "poses": poses}


sample_step = 0.125
plane_pairs = ((0, 1), (0, 2), (1, 2))

def smooth_weight(fraction):
    return fraction * fraction * (3.0 - 2.0 * fraction)

def lookup(planes_flat, points):
    summed = jnp.zeros((points.shape[1], planes_flat.shape[1]), jnp.float32)
    for plane_index, coord_pair in enumerate(plane_pairs):
        coord_u = points[coord_pair[0]] * P_SIZE
        coord_v = points[coord_pair[1]] * P_SIZE
        floor_u = jnp.floor(coord_u)
        floor_v = jnp.floor(coord_v)
        weight_u = smooth_weight(coord_u - floor_u)[:, None]
        weight_v = smooth_weight(coord_v - floor_v)[:, None]
        low_u = jnp.mod(floor_u.astype(jnp.int32), P_SIZE)
        low_v = jnp.mod(floor_v.astype(jnp.int32), P_SIZE)
        high_u = jnp.mod(low_u + 1, P_SIZE)
        high_v = jnp.mod(low_v + 1, P_SIZE)
        plane_base = plane_index * P_SIZE * P_SIZE
        corner_aa = planes_flat[plane_base + low_u * P_SIZE + low_v]
        corner_ab = planes_flat[plane_base + low_u * P_SIZE + high_v]
        corner_ba = planes_flat[plane_base + high_u * P_SIZE + low_v]
        corner_bb = planes_flat[plane_base + high_u * P_SIZE + high_v]
        summed = summed + (1.0 - weight_u) * ((1.0 - weight_v) * corner_aa + weight_v * corner_ab) + weight_u * ((1.0 - weight_v) * corner_ba + weight_v * corner_bb)
    return summed

def brick_samples(planes_flat, first_weight, hidden_weight, feature_weight, density_weight, received):
    sources, slot_total, flat_width = received.shape
    points = received.reshape(sources * slot_total, 3, S).transpose(1, 0, 2).reshape(3, -1)
    features = lookup(planes_flat, points).astype(jnp.bfloat16)
    hidden = jax.nn.silu(jnp.dot(features, first_weight.astype(jnp.bfloat16), preferred_element_type=jnp.float32)).astype(jnp.bfloat16)
    for layer_index in range(hidden_weight.shape[0]):
        hidden = jax.nn.silu(jnp.dot(hidden, hidden_weight[layer_index].astype(jnp.bfloat16), preferred_element_type=jnp.float32)).astype(jnp.bfloat16)
    colors = jnp.tanh(jnp.dot(hidden, feature_weight.astype(jnp.bfloat16), preferred_element_type=jnp.float32))
    density = jax.nn.softplus(jnp.dot(hidden, density_weight.astype(jnp.bfloat16), preferred_element_type=jnp.float32))
    return (colors.reshape(sources, slot_total, -1), density.reshape(sources, slot_total, S))

def composite(density, colors):
    optical_depth = density * sample_step
    before = jnp.cumsum(optical_depth, axis=-1) - optical_depth
    weight = jnp.exp(-before) * (1.0 - jnp.exp(-optical_depth))
    feature = lax.optimization_barrier(jnp.sum(weight[..., None] * colors, axis=-2))
    passing = jnp.exp(-lax.optimization_barrier(jnp.sum(optical_depth, axis=-1)))
    return (feature, passing)

def brick_segments(planes_flat, first_weight, hidden_weight, feature_weight, density_weight, received):
    colors, density = brick_samples(planes_flat, first_weight, hidden_weight, feature_weight, density_weight, received)
    sources, slot_total, flat_width = colors.shape
    return composite(density, colors.reshape(sources, slot_total, S, -1))

def ray_composite(segment_feature, segment_pass, brick_rank):
    transmit = jnp.ones(segment_pass.shape, segment_pass.dtype)
    for other_seg in range(K):
        in_front = brick_rank[:, other_seg][:, None] < brick_rank
        transmit = transmit * jnp.where(in_front, segment_pass[:, other_seg][:, None], 1.0)
    return lax.optimization_barrier(jnp.sum(transmit[:, :, None] * segment_feature, axis=1))

def cross_rows(left, right):
    return jnp.stack([left[1] * right[2] - left[2] * right[1], left[2] * right[0] - left[0] * right[2], left[0] * right[1] - left[1] * right[0]])

def sample_points(anchors, directions, ray_start, ray_pose, brick_rank):
    rotation = ray_pose[0:3]
    offset = ray_pose[3:6]
    moved_anchor = anchors + cross_rows(rotation, anchors) + offset
    moved_direction = directions + cross_rows(rotation, directions)
    place_along = brick_rank.astype(jnp.float32)[:, :, None] * S + jnp.arange(S)[None, None, :] + 0.5
    distance = ray_start[:, None, None] + place_along * sample_step
    return moved_anchor[:, :, None, None] + distance[None] * moved_direction[:, :, None, None]

def slot_numbers(target_brick, brick_count):
    onehot = (target_brick[:, None] == jnp.arange(brick_count)[None, :]).astype(jnp.int32)
    before = jnp.cumsum(onehot, axis=0) - onehot
    return lax.optimization_barrier(jnp.sum(before * onehot, axis=1)).astype(jnp.int32)

def reference(anchors, directions, ray_start, camera_ids, brick_ids, brick_rank, targets, planes, first_weight, hidden_weight, feature_weight, density_weight, poses):
    ray_count = anchors.shape[1]
    per_device = ray_count // BRICKS
    selector = (jnp.arange(NCAM)[:, None] == camera_ids[None, :]).astype(jnp.float32)

    def place(pose_table):
        ray_pose = jnp.dot(pose_table, selector, precision=lax.Precision.HIGHEST)
        return sample_points(anchors, directions, ray_start, ray_pose, brick_rank)
    points, pose_pullback = jax.vjp(place, poses)
    payload = points.transpose(1, 2, 0, 3).reshape(ray_count * K, 3 * S)
    target_brick = brick_ids.reshape(BRICKS, per_device * K).astype(jnp.int32)

    def per_row(row_bricks):
        return slot_numbers(row_bricks, BRICKS)
    slot_table = jax.vmap(per_row)(target_brick)
    source_dev = jnp.arange(BRICKS).astype(jnp.int32)[:, None]
    flat_slot = (target_brick * (BRICKS * CAP) + source_dev * CAP + slot_table).reshape(-1).astype(jnp.int32)
    incoming = jnp.zeros((BRICKS * BRICKS * CAP, 3 * S), jnp.float32).at[flat_slot].set(payload)
    incoming = incoming.reshape(BRICKS, BRICKS, CAP, 3 * S)
    stacked = (planes, first_weight, hidden_weight, feature_weight, density_weight)

    def forward_one(pieces):
        return brick_segments(pieces[0], pieces[1], pieces[2], pieces[3], pieces[4], pieces[5])
    seg_values, seg_optical = lax.map(forward_one, stacked + (incoming,))
    segment_values = seg_values.reshape(-1, C)[flat_slot]
    segment_optical = seg_optical.reshape(-1)[flat_slot]

    def ray_from(values_part, optical_part):
        return ray_composite(values_part.reshape(ray_count, K, C), optical_part.reshape(ray_count, K), brick_rank)
    ray_feature, ray_pullback = jax.vjp(ray_from, segment_values, segment_optical)
    values_grad, optical_grad = ray_pullback(ray_feature - targets)
    values_back = jnp.zeros((BRICKS * BRICKS * CAP, C), jnp.float32).at[flat_slot].set(values_grad).reshape(BRICKS, BRICKS, CAP, C)
    optical_back = jnp.zeros((BRICKS * BRICKS * CAP,), jnp.float32).at[flat_slot].set(optical_grad).reshape(BRICKS, BRICKS, CAP)

    def backward_one(pieces):
        outputs_unused, pullback = jax.vjp(brick_segments, pieces[0], pieces[1], pieces[2], pieces[3], pieces[4], pieces[5])
        return pullback((pieces[6], pieces[7]))
    gradients = lax.map(backward_one, stacked + (incoming, values_back, optical_back))
    point_grad = gradients[5].reshape(-1, 3 * S)[flat_slot].reshape(ray_count, K, 3, S).transpose(2, 0, 1, 3)
    pose_grad = pose_pullback(point_grad)[0]
    return (ray_feature, gradients[0], gradients[1], gradients[2], gradients[3], gradients[4], pose_grad)
```

```python
import functools

import jax
import jax.numpy as jnp
from jax import lax
from jax.experimental import pallas as pl
from jax.experimental.pallas import tpu as pltpu
from jax.sharding import PartitionSpec as P

SIDE = 64
STEP = 0.125
WIDTH = 128
AXES = ("gx", "gy")
BF16 = jnp.bfloat16
F32 = jnp.float32
MESH_ID = pl.DeviceIdType.MESH
VMEM_BYTES = 56 * 1024 * 1024


def dot(left, right, left_dim=1, right_dim=0, precision=None):
    return lax.dot_general(
        left,
        right,
        (((left_dim,), (right_dim,)), ((), ())),
        precision=precision,
        preferred_element_type=F32,
    )


def exact_dot(left, right, left_dim=1, right_dim=0):
    return dot(left, right, left_dim, right_dim, lax.Precision.HIGHEST)


def peer_id(index):
    side = lax.axis_size("gy")
    return (index // side, index % side)


def my_index():
    return lax.axis_index("gx") * lax.axis_size("gy") + lax.axis_index("gy")


def enter(count):
    me = my_index()
    barrier = pltpu.get_barrier_semaphore()

    def greet(step, carry):
        pl.semaphore_signal(
            barrier, inc=1, device_id=peer_id((me + step) % count), device_id_type=MESH_ID
        )
        return carry

    lax.fori_loop(1, count, greet, 0)
    pl.semaphore_wait(barrier, count - 1)


def rows_of(ref, index, rows):
    return ref.at[pl.ds(pl.multiple_of(index * rows, 8), rows)]


def remote_copy(count, step, source, target, rows, send_sem, recv_sem, shared):
    me = my_index()
    peer = (me + step) % count
    return pltpu.make_async_remote_copy(
        src_ref=source if shared else rows_of(source, peer, rows),
        dst_ref=rows_of(target, me, rows),
        send_sem=send_sem.at[step],
        recv_sem=recv_sem.at[me],
        device_id=peer_id(peer),
        device_id_type=MESH_ID,
    )


def send_all(count, source, target, rows, send_sem, recv_sem, shared=False):
    def send(step, carry):
        remote_copy(count, step, source, target, rows, send_sem, recv_sem, shared).start()
        return carry

    lax.fori_loop(1, count, send, 0)


def wait_all(count, source, target, rows, send_sem, recv_sem, shared=False):
    me = my_index()

    def arrive(step, carry):
        origin = (me + count - step) % count
        pltpu.make_async_remote_copy(
            src_ref=source if shared else rows_of(source, origin, rows),
            dst_ref=rows_of(target, origin, rows),
            send_sem=send_sem.at[step],
            recv_sem=recv_sem.at[origin],
            device_id=peer_id(origin),
            device_id_type=MESH_ID,
        ).wait_recv()
        return carry

    lax.fori_loop(1, count, arrive, 0)

    def leave(step, carry):
        remote_copy(count, step, source, target, rows, send_sem, recv_sem, shared).wait_send()
        return carry

    lax.fori_loop(1, count, leave, 0)


def keep_own(source, target, rows):
    here = pl.ds(pl.multiple_of(my_index() * rows, 8), rows)
    target[here, :] = source[here, :]


def points_kernel(count, rows, sent, received, landed, send_sem, recv_sem):
    enter(count)
    send_all(count, sent, landed, rows, send_sem, recv_sem)
    keep_own(sent, landed, rows)
    wait_all(count, sent, landed, rows, send_sem, recv_sem)
    received[...] = landed[...]


def owner_kernel(
    count,
    rows,
    ray_count,
    segs,
    sent,
    route,
    route_back,
    ranks,
    targets,
    ray_out,
    received,
    home,
    outgoing,
    landed,
    send_sem,
    recv_sem,
    send_sem2,
    recv_sem2,
):
    enter(count)
    send_all(count, sent, home, rows, send_sem, recv_sem)
    keep_own(sent, home, rows)
    wait_all(count, sent, home, rows, send_sem, recv_sem)
    listed = exact_dot(route[...], home[...])
    feature = [listed[k * ray_count : (k + 1) * ray_count, :WIDTH] for k in range(segs)]
    passing = [listed[k * ray_count : (k + 1) * ray_count, WIDTH:] for k in range(segs)]
    rank = [
        jnp.broadcast_to(ranks[:, k : k + 1], (ray_count, WIDTH)).astype(F32)
        for k in range(segs)
    ]

    def through(k, skipped):
        product = jnp.ones((ray_count, WIDTH), F32)
        for other in range(segs):
            if other != k and other != skipped:
                product = product * jnp.where(rank[other] < rank[k], passing[other], 1.0)
        return product

    transmit = [through(k, k) for k in range(segs)]
    ray = transmit[0] * feature[0]
    for k in range(1, segs):
        ray = ray + transmit[k] * feature[k]
    ray_out[...] = ray
    residual = ray - targets[...]
    along = [jnp.sum(residual * feature[k], axis=1, keepdims=True) for k in range(segs)]
    back = []
    for k in range(segs):
        pass_grad = jnp.zeros((ray_count, WIDTH), F32)
        for behind in range(segs):
            if behind != k:
                pass_grad = pass_grad + jnp.where(
                    rank[k] < rank[behind], through(behind, k) * along[behind], 0.0
                )
        back.append(jnp.concatenate([transmit[k] * residual, pass_grad], axis=1))
    outgoing[...] = exact_dot(route_back[...], jnp.concatenate(back, axis=0))
    send_all(count, outgoing, landed, rows, send_sem2, recv_sem2)
    keep_own(outgoing, landed, rows)
    wait_all(count, outgoing, landed, rows, send_sem2, recv_sem2)
    received[...] = landed[...]


def pose_kernel(count, rows, own, total, landed, send_sem, recv_sem):
    enter(count)
    send_all(count, own, landed, rows, send_sem, recv_sem, shared=True)
    here = pl.ds(pl.multiple_of(my_index() * rows, 8), rows)
    landed[here, :] = own[...]
    wait_all(count, own, landed, rows, send_sem, recv_sem, shared=True)
    summed = landed[0:rows, :]
    for index in range(1, count):
        summed = summed + landed[index * rows : (index + 1) * rows, :]
    total[...] = summed


def coordinate_rows(payload, samples):
    columns = payload.T
    return [
        jnp.concatenate([columns[c * samples + s : c * samples + s + 1] for s in range(samples)], 1)
        for c in range(3)
    ]


def fill_factors(coords, factor, slope=None):
    total = coords[0].shape[1]
    cells = lax.broadcasted_iota(jnp.int32, (SIDE, total), 0)
    for c in range(3):
        scaled = coords[c] * float(SIDE)
        floor_c = jnp.floor(scaled)
        fraction = scaled - floor_c
        weight = fraction * fraction * (3.0 - 2.0 * fraction)
        low = floor_c.astype(jnp.int32) & (SIDE - 1)
        high = (low + 1) & (SIDE - 1)
        low_hit = cells == low
        high_hit = cells == high
        factor[c] = jnp.where(low_hit, 1.0 - weight, jnp.where(high_hit, weight, 0.0))
        if slope is not None:
            change = float(SIDE) * 6.0 * fraction * (1.0 - fraction)
            slope[c] = jnp.where(low_hit, -change, jnp.where(high_hit, change, 0.0))


def block_place(lines):
    plane, block = pl.program_id(0), pl.program_id(1)
    return plane // 2, (plane + 3) // 2, block * lines


def fill_table(factor, table, lines):
    row_axis, col_axis, first = block_place(lines)

    def one(line, carry):
        row = factor[row_axis, pl.ds(first + line, 1), :]
        table[pl.ds(pl.multiple_of(line * SIDE, SIDE), SIDE), :] = (
            row * factor[col_axis]
        ).astype(BF16)
        return carry

    lax.fori_loop(0, lines, one, 0)


def network(features, first, hidden, heads):
    pre1 = dot(features, first)
    gate1 = jax.nn.sigmoid(pre1)
    hidden1 = (pre1 * gate1).astype(BF16)
    pre2 = dot(hidden1, hidden)
    gate2 = jax.nn.sigmoid(pre2)
    hidden2 = (pre2 * gate2).astype(BF16)
    last = dot(hidden2, heads)
    colors = jnp.tanh(last[:, :WIDTH])
    raw = last[:, WIDTH:]
    density = jnp.maximum(raw, 0.0) + jnp.log1p(jnp.exp(-jnp.abs(raw)))
    return pre1, gate1, hidden1, pre2, gate2, hidden2, colors, raw, density


def transmittance(density, samples):
    rows = density.shape[0] // samples
    depth = [density[s * rows : (s + 1) * rows] * STEP for s in range(samples)]
    before = jnp.zeros_like(depth[0])
    reach, kept = [], []
    for s in range(samples):
        reach.append(jnp.exp(-before))
        kept.append(jnp.exp(-depth[s]))
        before = before + depth[s]
    return reach, kept, jnp.exp(-before)


def last_step():
    return (pl.program_id(0) == pl.num_programs(0) - 1) & (
        pl.program_id(1) == pl.num_programs(1) - 1
    )


def first_step():
    return (pl.program_id(0) == 0) & (pl.program_id(1) == 0)


def forward_kernel(
    samples, lines, payload, planes, first, hidden, heads, message, features, factor, table, summed
):
    @pl.when(first_step())
    def _():
        fill_factors(coordinate_rows(payload[...], samples), factor)
        summed[...] = jnp.zeros_like(summed)

    fill_table(factor, table, lines)
    summed[...] += dot(planes[0].T.astype(BF16), table[...])

    @pl.when(last_step())
    def _():
        rounded = summed[...].T.astype(BF16)
        features[...] = rounded
        parts = network(rounded, first[...], hidden[...], heads[...])
        colors, density = parts[6], parts[8]
        reach, kept, passing = transmittance(density, samples)
        rows = passing.shape[0]
        value = jnp.zeros_like(passing)
        for s in range(samples):
            value = value + reach[s] * (1.0 - kept[s]) * colors[s * rows : (s + 1) * rows]
        message[:, :WIDTH] = value
        message[:, WIDTH:] = passing


def silu_slope(pre, gate):
    return gate * (1.0 + pre * (1.0 - gate))


def backward_kernel(
    samples,
    lines,
    payload,
    planes,
    first,
    hidden,
    heads,
    features,
    incoming,
    plane_grad,
    first_grad,
    hidden_grad,
    heads_grad,
    pose_grad,
    factor,
    slope,
    table,
    cot,
    point_grad,
):
    @pl.when(first_step())
    def _():
        fill_factors(coordinate_rows(payload[...], samples), factor, slope)
        point_grad[...] = jnp.zeros_like(point_grad)
        pre1, gate1, hidden1, pre2, gate2, hidden2, colors, raw, density = network(
            features[...], first[...], hidden[...], heads[...]
        )
        reach, kept, passing = transmittance(density, samples)
        rows = passing.shape[0]
        feature_cot = incoming[:, :WIDTH]
        pass_cot = incoming[:, WIDTH:] * passing
        behind = pass_cot
        color_cots = [None] * samples
        depth_cots = [None] * samples
        for s in reversed(range(samples)):
            here = colors[s * rows : (s + 1) * rows]
            along = jnp.sum(feature_cot * here, axis=1, keepdims=True)
            weight = reach[s] * (1.0 - kept[s])
            color_cots[s] = weight * feature_cot * (1.0 - here * here)
            depth_cots[s] = along * reach[s] * kept[s] - behind
            behind = behind + along * weight
        raw_cot = jnp.concatenate(depth_cots, axis=0) * STEP * jax.nn.sigmoid(raw)
        lane = lax.broadcasted_iota(jnp.int32, raw_cot.shape, 1)
        raw_cot = jnp.where(lane == 0, raw_cot, 0.0)
        last_cot = jnp.concatenate([jnp.concatenate(color_cots, axis=0), raw_cot], axis=1)
        last_cot = last_cot.astype(BF16)
        heads_grad[...] = dot(hidden2, last_cot, 0, 0).astype(BF16).astype(F32)
        cot2 = dot(last_cot, heads[...], 1, 1).astype(BF16).astype(F32)
        cot2 = (cot2 * silu_slope(pre2, gate2)).astype(BF16)
        hidden_grad[...] = dot(hidden1, cot2, 0, 0).astype(BF16).astype(F32)
        cot1 = dot(cot2, hidden[...], 1, 1).astype(BF16).astype(F32)
        cot1 = (cot1 * silu_slope(pre1, gate1)).astype(BF16)
        first_grad[...] = dot(features[...], cot1, 0, 0).astype(BF16).astype(F32)
        cot[...] = dot(cot1, first[...], 1, 1).astype(BF16)

    fill_table(factor, table, lines)
    plane_grad[0] = dot(table[...], cot[...])
    row_axis, col_axis, first_line = block_place(lines)
    total = cot.shape[0]

    def one(line, carry):
        cells = planes[0, pl.ds(pl.multiple_of(line * SIDE, SIDE), SIDE), :].astype(BF16)
        product = dot(cells, cot[...], 1, 1)
        by_col = (product * factor[col_axis]).reshape(SIDE // 8, 8, total).sum(0)
        by_slope = (product * slope[col_axis]).reshape(SIDE // 8, 8, total).sum(0)
        row = pl.ds(first_line + line, 1)
        point_grad[row_axis] += by_col * slope[row_axis, row, :]
        point_grad[col_axis] += by_slope * factor[row_axis, row, :]
        return carry

    lax.fori_loop(0, lines, one, 0)

    @pl.when(last_step())
    def _():
        columns = payload[...].T
        rows = columns.shape[1]
        base = 3 * samples
        anchor = [columns[base + c : base + c + 1] for c in range(3)]
        direction = [columns[base + 3 + c : base + 4 + c] for c in range(3)]
        place_grad, way_grad = [], []
        for c in range(3):
            whole = jnp.sum(point_grad[c], axis=0, keepdims=True)
            place = jnp.zeros((1, rows), F32)
            way = jnp.zeros((1, rows), F32)
            for s in range(samples):
                piece = whole[:, s * rows : (s + 1) * rows]
                place = place + piece
                way = way + piece * columns[base + 6 + s : base + 7 + s]
            place_grad.append(place)
            way_grad.append(way)
        turn = []
        for c in range(3):
            d, e = (c + 1) % 3, (c + 2) % 3
            turn.append(
                anchor[d] * place_grad[e]
                - anchor[e] * place_grad[d]
                + direction[d] * way_grad[e]
                - direction[e] * way_grad[d]
            )
        stacked = jnp.concatenate(turn + place_grad + [jnp.zeros((2, rows), F32)], axis=0)
        camera = payload[:, base + 6 + samples : base + 7 + samples]
        cameras = pose_grad.shape[1]
        named = lax.broadcasted_iota(jnp.int32, (rows, cameras), 1).astype(F32) == camera
        pose_grad[...] = exact_dot(stacked, named.astype(F32))


def cross_rows(left, right):
    return jnp.stack(
        [
            left[1] * right[2] - left[2] * right[1],
            left[2] * right[0] - left[0] * right[2],
            left[0] * right[1] - left[1] * right[0],
        ]
    )


def slot_numbers(target_brick, brick_count):
    onehot = (target_brick[:, None] == jnp.arange(brick_count)[None, :]).astype(F32)
    rows = target_brick.shape[0]
    lower = (jnp.arange(rows)[:, None] > jnp.arange(rows)[None, :]).astype(F32)
    before = jnp.dot(lower, onehot, preferred_element_type=F32)
    return jnp.sum(before * onehot, axis=1).astype(jnp.int32)


def whole_spec(shape):
    return pl.BlockSpec(shape, lambda *place: (0,) * len(shape))


def shaped(*shape):
    return jax.ShapeDtypeStruct(shape, F32)


def remote_params(number):
    return pltpu.CompilerParams(
        collective_id=number, has_side_effects=True, vmem_limit_bytes=VMEM_BYTES
    )


def per_device(
    anchors,
    directions,
    ray_start,
    camera_ids,
    brick_ids,
    brick_rank,
    targets,
    planes,
    first_weight,
    hidden_weight,
    feature_weight,
    density_weight,
    poses,
):
    count = lax.axis_size(AXES)
    ray_count, segs = brick_ids.shape
    samples = 4
    cap = 2 * ray_count * segs // count
    rows = -(-cap // 8) * 8
    listed = ray_count * segs
    slots = count * cap
    total = slots * samples
    cameras = poses.shape[1]
    in_vmem = pl.BlockSpec(memory_space=pltpu.VMEM)

    selector = (jnp.arange(cameras)[:, None] == camera_ids[None, :]).astype(F32)
    ray_pose = jnp.dot(poses, selector, precision=lax.Precision.HIGHEST)
    moved_anchor = anchors + cross_rows(ray_pose[0:3], anchors) + ray_pose[3:6]
    moved_direction = directions + cross_rows(ray_pose[0:3], directions)
    along = brick_rank.T.astype(F32)[:, :, None] * samples + jnp.arange(samples) + 0.5
    distance = ray_start[None, :, None] + along * STEP
    points = moved_anchor.T[None, :, :, None] + distance[:, :, None, :] * (
        moved_direction.T[None, :, :, None]
    )
    per_ray = jnp.concatenate([anchors.T, directions.T], axis=1)
    payload = jnp.concatenate(
        [
            points.reshape(listed, 3 * samples),
            jnp.tile(per_ray, (segs, 1)),
            distance.reshape(listed, samples),
            jnp.tile(camera_ids.astype(F32)[:, None], (segs, 1)),
        ],
        axis=1,
    )
    payload = jnp.pad(payload, ((0, 0), (0, WIDTH - payload.shape[1])))
    target_brick = brick_ids.T.reshape(-1)
    slot = target_brick * rows + slot_numbers(target_brick, count)
    slot_range = jnp.arange(count * rows)
    route = (slot[:, None] == slot_range[None, :]).astype(F32)
    route_back = (slot_range[:, None] == slot[None, :]).astype(F32)
    outgoing = jnp.dot(route_back, payload, precision=lax.Precision.HIGHEST)

    def narrow(padded):
        if rows == cap:
            return padded
        return padded.reshape(count, rows, -1)[:, :cap].reshape(slots, -1)

    def widen(packed):
        if rows == cap:
            return packed
        grouped = packed.reshape(count, cap, -1)
        return jnp.pad(grouped, ((0, 0), (0, rows - cap), (0, 0))).reshape(count * rows, -1)

    pair = [pltpu.SemaphoreType.DMA((count,)), pltpu.SemaphoreType.DMA((count,))]
    received = pl.pallas_call(
        functools.partial(points_kernel, count, rows),
        out_shape=shaped(count * rows, WIDTH),
        in_specs=[in_vmem],
        out_specs=in_vmem,
        scratch_shapes=[pltpu.VMEM((count * rows, WIDTH), F32)] + pair,
        compiler_params=remote_params(0),
        name="send_points",
    )(outgoing)
    received = narrow(received)

    first = first_weight[0].astype(BF16)
    hidden = hidden_weight[0, 0].astype(BF16)
    heads = jnp.concatenate(
        [feature_weight[0], jnp.broadcast_to(density_weight[0][:, None], feature_weight[0].shape)],
        axis=1,
    ).astype(BF16)
    channels = planes.shape[2]
    lines = 16
    cells = lines * SIDE
    grid = (3, SIDE // lines)
    plane_spec = pl.BlockSpec((1, cells, channels), lambda q, i: (0, q * (SIDE // lines) + i, 0))
    local = pltpu.CompilerParams(vmem_limit_bytes=VMEM_BYTES)
    message, features = pl.pallas_call(
        functools.partial(forward_kernel, samples, lines),
        grid=grid,
        out_shape=[shaped(slots, 2 * WIDTH), jax.ShapeDtypeStruct((total, channels), BF16)],
        in_specs=[whole_spec(received.shape), plane_spec]
        + [whole_spec(w.shape) for w in (first, hidden, heads)],
        out_specs=[whole_spec((slots, 2 * WIDTH)), whole_spec((total, channels))],
        scratch_shapes=[
            pltpu.VMEM((3, SIDE, total), F32),
            pltpu.VMEM((cells, total), BF16),
            pltpu.VMEM((channels, total), F32),
        ],
        compiler_params=local,
        name="brick_forward",
    )(received, planes, first, hidden, heads)

    wide = (count * rows, 2 * WIDTH)
    ray_feature, incoming = pl.pallas_call(
        functools.partial(owner_kernel, count, rows, ray_count, segs),
        out_shape=[shaped(ray_count, WIDTH), shaped(*wide)],
        in_specs=[in_vmem] * 5,
        out_specs=[in_vmem] * 2,
        scratch_shapes=[pltpu.VMEM(wide, F32)] * 3 + pair + pair,
        compiler_params=remote_params(1),
        name="rays",
    )(widen(message), route, route_back, brick_rank, targets)
    incoming = narrow(incoming)

    plane_grad, first_grad, hidden_grad, heads_grad, pose_local = pl.pallas_call(
        functools.partial(backward_kernel, samples, lines),
        grid=grid,
        out_shape=[
            jax.ShapeDtypeStruct(planes.shape, F32),
            shaped(*first.shape),
            shaped(*hidden.shape),
            shaped(*heads.shape),
            shaped(8, cameras),
        ],
        in_specs=[whole_spec(received.shape), plane_spec]
        + [whole_spec(w.shape) for w in (first, hidden, heads, features, incoming)],
        out_specs=[plane_spec]
        + [whole_spec(w.shape) for w in (first, hidden, heads)]
        + [whole_spec((8, cameras))],
        scratch_shapes=[
            pltpu.VMEM((3, SIDE, total), F32),
            pltpu.VMEM((3, SIDE, total), F32),
            pltpu.VMEM((cells, total), BF16),
            pltpu.VMEM((total, channels), BF16),
            pltpu.VMEM((3, 8, total), F32),
        ],
        compiler_params=local,
        name="brick_backward",
    )(received, planes, first, hidden, heads, features, incoming)

    pose_grad = pl.pallas_call(
        functools.partial(pose_kernel, count, 8),
        out_shape=shaped(8, cameras),
        in_specs=[in_vmem],
        out_specs=in_vmem,
        scratch_shapes=[pltpu.VMEM((count * 8, cameras), F32)] + pair,
        compiler_params=remote_params(2),
        name="sum_poses",
    )(pose_local)[:6]
    return (
        ray_feature,
        plane_grad,
        first_grad[None],
        hidden_grad[None, None],
        heads_grad[None, :, :WIDTH],
        heads_grad[None, :, WIDTH],
        pose_grad,
    )


def solution(mesh):
    split = P(AXES)
    in_specs = (P(None, AXES), P(None, AXES)) + (split,) * 10 + (P(),)
    out_specs = (split,) * 6 + (P(),)
    return jax.shard_map(
        per_device, mesh=mesh, in_specs=in_specs, out_specs=out_specs, check_vma=False
    )
```

```python
import functools

import jax
import jax.numpy as jnp
from jax import lax
from jax.experimental import pallas as pl
from jax.experimental.pallas import tpu as pltpu
from jax.sharding import PartitionSpec as P

SIDE = 64
STEP = 0.125
WIDTH = 128
AXES = ("gx", "gy")
BF16 = jnp.bfloat16
F32 = jnp.float32
MESH_ID = pl.DeviceIdType.MESH
VMEM_BYTES = 56 * 1024 * 1024


def dot(left, right, left_dim=1, right_dim=0, precision=None):
    return lax.dot_general(
        left,
        right,
        (((left_dim,), (right_dim,)), ((), ())),
        precision=precision,
        preferred_element_type=F32,
    )


def exact_dot(left, right, left_dim=1, right_dim=0):
    return dot(left, right, left_dim, right_dim, lax.Precision.HIGHEST)


def peer_id(index):
    side = lax.axis_size("gy")
    return (index // side, index % side)


def my_index():
    return lax.axis_index("gx") * lax.axis_size("gy") + lax.axis_index("gy")


def enter(count):
    me = my_index()
    barrier = pltpu.get_barrier_semaphore()

    def greet(step, carry):
        pl.semaphore_signal(
            barrier, inc=1, device_id=peer_id((me + step) % count), device_id_type=MESH_ID
        )
        return carry

    lax.fori_loop(1, count, greet, 0)


def all_entered(count):
    pl.semaphore_wait(pltpu.get_barrier_semaphore(), count - 1)


def rows_of(ref, index, rows):
    return ref.at[pl.ds(pl.multiple_of(index * rows, 8), rows)]


def remote_copy(count, step, source, target, rows, send_sem, recv_sem, shared):
    me = my_index()
    peer = (me + step) % count
    return pltpu.make_async_remote_copy(
        src_ref=source if shared else rows_of(source, peer, rows),
        dst_ref=rows_of(target, me, rows),
        send_sem=send_sem.at[step],
        recv_sem=recv_sem.at[me],
        device_id=peer_id(peer),
        device_id_type=MESH_ID,
    )


def send_all(count, source, target, rows, send_sem, recv_sem, shared=False):
    def send(step, carry):
        remote_copy(count, step, source, target, rows, send_sem, recv_sem, shared).start()
        return carry

    lax.fori_loop(1, count, send, 0)


def wait_all(count, source, target, rows, send_sem, recv_sem, shared=False):
    me = my_index()

    def arrive(step, carry):
        origin = (me + count - step) % count
        pltpu.make_async_remote_copy(
            src_ref=source if shared else rows_of(source, origin, rows),
            dst_ref=rows_of(target, origin, rows),
            send_sem=send_sem.at[step],
            recv_sem=recv_sem.at[origin],
            device_id=peer_id(origin),
            device_id_type=MESH_ID,
        ).wait_recv()
        return carry

    lax.fori_loop(1, count, arrive, 0)

    def leave(step, carry):
        remote_copy(count, step, source, target, rows, send_sem, recv_sem, shared).wait_send()
        return carry

    lax.fori_loop(1, count, leave, 0)


def keep_own(source, target, rows):
    here = pl.ds(pl.multiple_of(my_index() * rows, 8), rows)
    target[here, :] = source[here, :]


def cross_rows(left, right):
    return [
        left[1] * right[2] - left[2] * right[1],
        left[2] * right[0] - left[0] * right[2],
        left[0] * right[1] - left[1] * right[0],
    ]


def row_list(array, start, number):
    return [array[start + c : start + c + 1] for c in range(number)]


def points_kernel(
    count, rows, samples, listing, poses, received, route_out, sent, landed, send_sem, recv_sem
):
    enter(count)
    listed = listing.shape[1]
    anchors = row_list(listing, 0, 3)
    directions = row_list(listing, 3, 3)
    ray_start, camera, rank, brick = row_list(listing, 6, 4)
    cameras = lax.broadcasted_iota(jnp.int32, (poses.shape[1], listed), 0).astype(F32)
    ray_pose = exact_dot(poses[...], (cameras == camera).astype(F32))
    turned_anchor = cross_rows(row_list(ray_pose, 0, 3), anchors)
    turned_direction = cross_rows(row_list(ray_pose, 0, 3), directions)
    moved_anchor = [anchors[c] + turned_anchor[c] + ray_pose[3 + c : 4 + c] for c in range(3)]
    moved_direction = [directions[c] + turned_direction[c] for c in range(3)]
    distance = [ray_start + (rank * samples + s + 0.5) * STEP for s in range(samples)]
    payload = [
        moved_anchor[c] + distance[s] * moved_direction[c]
        for c in range(3)
        for s in range(samples)
    ]
    payload = payload + anchors + directions + distance + [camera]
    filler = jnp.zeros((WIDTH - len(payload), listed), F32)
    payload = jnp.concatenate(payload + [filler], axis=0)
    bricks = lax.broadcasted_iota(jnp.int32, (count, listed), 0).astype(F32)
    named = (bricks == brick).astype(F32)
    earlier = lax.broadcasted_iota(jnp.int32, (listed, listed), 0)
    later = lax.broadcasted_iota(jnp.int32, (listed, listed), 1)
    before = dot(named.astype(BF16), (earlier < later).astype(BF16))
    slot = brick * rows + jnp.sum(before * named, axis=0, keepdims=True)
    slots = lax.broadcasted_iota(jnp.int32, (count * rows, listed), 0).astype(F32)
    route = (slots == slot).astype(F32)
    route_out[...] = route
    sent[...] = exact_dot(route, payload, 1, 1)
    all_entered(count)
    send_all(count, sent, landed, rows, send_sem, recv_sem)
    keep_own(sent, landed, rows)
    wait_all(count, sent, landed, rows, send_sem, recv_sem)
    received[...] = landed[...]


def owner_kernel(
    count,
    rows,
    ray_count,
    segs,
    sent,
    route,
    ranks,
    targets,
    ray_out,
    received,
    home,
    outgoing,
    landed,
    send_sem,
    recv_sem,
    send_sem2,
    recv_sem2,
):
    enter(count)
    all_entered(count)
    send_all(count, sent, home, rows, send_sem, recv_sem)
    keep_own(sent, home, rows)
    wait_all(count, sent, home, rows, send_sem, recv_sem)
    listed = exact_dot(route[...], home[...], 0, 0)
    feature = [listed[k * ray_count : (k + 1) * ray_count, :WIDTH] for k in range(segs)]
    passing = [listed[k * ray_count : (k + 1) * ray_count, WIDTH:] for k in range(segs)]
    rank = [
        jnp.broadcast_to(ranks[:, k : k + 1], (ray_count, WIDTH)).astype(F32)
        for k in range(segs)
    ]

    def through(k, skipped):
        product = jnp.ones((ray_count, WIDTH), F32)
        for other in range(segs):
            if other != k and other != skipped:
                product = product * jnp.where(rank[other] < rank[k], passing[other], 1.0)
        return product

    transmit = [through(k, k) for k in range(segs)]
    ray = transmit[0] * feature[0]
    for k in range(1, segs):
        ray = ray + transmit[k] * feature[k]
    ray_out[...] = ray
    residual = ray - targets[...]
    along = [jnp.sum(residual * feature[k], axis=1, keepdims=True) for k in range(segs)]
    back = []
    for k in range(segs):
        pass_grad = jnp.zeros((ray_count, WIDTH), F32)
        for behind in range(segs):
            if behind != k:
                pass_grad = pass_grad + jnp.where(
                    rank[k] < rank[behind], through(behind, k) * along[behind], 0.0
                )
        back.append(jnp.concatenate([transmit[k] * residual, pass_grad], axis=1))
    outgoing[...] = exact_dot(route[...], jnp.concatenate(back, axis=0))
    send_all(count, outgoing, landed, rows, send_sem2, recv_sem2)
    keep_own(outgoing, landed, rows)
    wait_all(count, outgoing, landed, rows, send_sem2, recv_sem2)
    received[...] = landed[...]


def pose_kernel(count, rows, own, total, landed, send_sem, recv_sem):
    enter(count)
    all_entered(count)
    send_all(count, own, landed, rows, send_sem, recv_sem, shared=True)
    here = pl.ds(pl.multiple_of(my_index() * rows, 8), rows)
    landed[here, :] = own[...]
    wait_all(count, own, landed, rows, send_sem, recv_sem, shared=True)
    summed = landed[0:rows, :]
    for index in range(1, count):
        summed = summed + landed[index * rows : (index + 1) * rows, :]
    total[...] = summed[: total.shape[0]]


def coordinate_rows(payload, samples):
    columns = payload.T
    return [
        jnp.concatenate([columns[c * samples + s : c * samples + s + 1] for s in range(samples)], 1)
        for c in range(3)
    ]


def fill_factors(coords, factor, slope=None):
    total = coords[0].shape[1]
    cells = lax.broadcasted_iota(jnp.int32, (SIDE, total), 0)
    for c in range(3):
        scaled = coords[c] * float(SIDE)
        floor_c = jnp.floor(scaled)
        fraction = scaled - floor_c
        weight = fraction * fraction * (3.0 - 2.0 * fraction)
        low = floor_c.astype(jnp.int32) & (SIDE - 1)
        high = (low + 1) & (SIDE - 1)
        low_hit = cells == low
        high_hit = cells == high
        factor[c] = jnp.where(low_hit, 1.0 - weight, jnp.where(high_hit, weight, 0.0))
        if slope is not None:
            change = float(SIDE) * 6.0 * fraction * (1.0 - fraction)
            slope[c] = jnp.where(low_hit, -change, jnp.where(high_hit, change, 0.0))


def block_place(lines):
    plane, block = pl.program_id(0), pl.program_id(1)
    return plane // 2, (plane + 3) // 2, block * lines


def fill_table(factor, table, lines):
    row_axis, col_axis, first = block_place(lines)

    def one(line, carry):
        row = factor[row_axis, pl.ds(first + line, 1), :]
        table[pl.ds(pl.multiple_of(line * SIDE, SIDE), SIDE), :] = (
            row * factor[col_axis]
        ).astype(BF16)
        return carry

    lax.fori_loop(0, lines, one, 0)


def bf16_weights(first, hidden, feature, density):
    column = jnp.broadcast_to(density[...], (WIDTH, density.shape[1])).T
    heads = jnp.concatenate([feature[0], column], axis=1).astype(BF16)
    return first[0].astype(BF16), hidden[0, 0].astype(BF16), heads


def network(features, first, hidden, heads):
    pre1 = dot(features, first)
    gate1 = jax.nn.sigmoid(pre1)
    hidden1 = (pre1 * gate1).astype(BF16)
    pre2 = dot(hidden1, hidden)
    gate2 = jax.nn.sigmoid(pre2)
    hidden2 = (pre2 * gate2).astype(BF16)
    last = dot(hidden2, heads)
    colors = jnp.tanh(last[:, :WIDTH])
    raw = last[:, WIDTH:]
    density = jnp.maximum(raw, 0.0) + jnp.log1p(jnp.exp(-jnp.abs(raw)))
    return pre1, gate1, hidden1, pre2, gate2, hidden2, colors, raw, density


def transmittance(density, samples):
    rows = density.shape[0] // samples
    depth = [density[s * rows : (s + 1) * rows] * STEP for s in range(samples)]
    before = jnp.zeros_like(depth[0])
    reach, kept = [], []
    for s in range(samples):
        reach.append(jnp.exp(-before))
        kept.append(jnp.exp(-depth[s]))
        before = before + depth[s]
    return reach, kept, jnp.exp(-before)


def last_step():
    return (pl.program_id(0) == pl.num_programs(0) - 1) & (
        pl.program_id(1) == pl.num_programs(1) - 1
    )


def first_step():
    return (pl.program_id(0) == 0) & (pl.program_id(1) == 0)


def forward_kernel(
    samples,
    lines,
    payload,
    planes,
    first,
    hidden,
    feature,
    density,
    message,
    features,
    factor,
    table,
    summed,
):
    @pl.when(first_step())
    def _():
        fill_factors(coordinate_rows(payload[...], samples), factor)
        summed[...] = jnp.zeros_like(summed)

    fill_table(factor, table, lines)
    summed[...] += dot(planes[0].T.astype(BF16), table[...])

    @pl.when(last_step())
    def _():
        rounded = summed[...].T.astype(BF16)
        features[...] = rounded
        parts = network(rounded, *bf16_weights(first, hidden, feature, density))
        colors = parts[6]
        reach, kept, passing = transmittance(parts[8], samples)
        rows = passing.shape[0]
        value = jnp.zeros_like(passing)
        for s in range(samples):
            value = value + reach[s] * (1.0 - kept[s]) * colors[s * rows : (s + 1) * rows]
        message[:, :WIDTH] = value
        message[:, WIDTH:] = passing


def silu_slope(pre, gate):
    return gate * (1.0 + pre * (1.0 - gate))


def backward_kernel(
    samples,
    lines,
    payload,
    planes,
    first,
    hidden,
    feature,
    density,
    features,
    incoming,
    plane_grad,
    first_grad,
    hidden_grad,
    feature_grad,
    density_grad,
    pose_grad,
    factor,
    slope,
    table,
    cot,
    cot_rows,
    product,
    point_grad,
):
    @pl.when(first_step())
    def _():
        fill_factors(coordinate_rows(payload[...], samples), factor, slope)
        point_grad[...] = jnp.zeros_like(point_grad)
        weight1, weight2, heads = bf16_weights(first, hidden, feature, density)
        pre1, gate1, hidden1, pre2, gate2, hidden2, colors, raw, thick = network(
            features[...], weight1, weight2, heads
        )
        reach, kept, passing = transmittance(thick, samples)
        rows = passing.shape[0]
        feature_cot = incoming[:, :WIDTH]
        pass_cot = incoming[:, WIDTH:] * passing
        behind = pass_cot
        color_cots = [None] * samples
        depth_cots = [None] * samples
        for s in reversed(range(samples)):
            here = colors[s * rows : (s + 1) * rows]
            along = jnp.sum(feature_cot * here, axis=1, keepdims=True)
            weight = reach[s] * (1.0 - kept[s])
            color_cots[s] = weight * feature_cot * (1.0 - here * here)
            depth_cots[s] = along * reach[s] * kept[s] - behind
            behind = behind + along * weight
        raw_cot = jnp.concatenate(depth_cots, axis=0) * STEP * jax.nn.sigmoid(raw)
        lane = lax.broadcasted_iota(jnp.int32, raw_cot.shape, 1)
        raw_cot = jnp.where(lane == 0, raw_cot, 0.0)
        last_cot = jnp.concatenate([jnp.concatenate(color_cots, axis=0), raw_cot], axis=1)
        last_cot = last_cot.astype(BF16)
        feature_grad[0] = dot(hidden2, last_cot[:, :WIDTH], 0, 0).astype(BF16).astype(F32)
        by_density = dot(last_cot[:, WIDTH:], hidden2, 0, 0)
        density_grad[...] = by_density[0:1].astype(BF16).astype(F32)
        cot2 = dot(last_cot, heads, 1, 1).astype(BF16).astype(F32)
        cot2 = (cot2 * silu_slope(pre2, gate2)).astype(BF16)
        hidden_grad[0, 0] = dot(hidden1, cot2, 0, 0).astype(BF16).astype(F32)
        cot1 = dot(cot2, weight2, 1, 1).astype(BF16).astype(F32)
        cot1 = (cot1 * silu_slope(pre1, gate1)).astype(BF16)
        first_grad[0] = dot(features[...], cot1, 0, 0).astype(BF16).astype(F32)
        sample_cot = dot(cot1, weight1, 1, 1)
        cot[...] = sample_cot.astype(BF16)
        cot_rows[...] = sample_cot.T.astype(BF16)

    fill_table(factor, table, lines)
    plane_grad[0] = dot(table[...], cot[...])
    row_axis, col_axis, first_line = block_place(lines)
    product[...] = dot(planes[0].astype(BF16), cot_rows[...])

    def one(chunk, carry):
        lanes = pl.ds(pl.multiple_of(chunk * WIDTH, WIDTH), WIDTH)
        col, col_slope = factor[col_axis, :, lanes], slope[col_axis, :, lanes]
        here = pl.ds(pl.multiple_of(first_line, 8), lines)
        rows, row_slopes = factor[row_axis, here, lanes], slope[row_axis, here, lanes]
        row_total = jnp.zeros((8, WIDTH), F32)
        col_total = jnp.zeros((8, WIDTH), F32)
        for line in range(lines):
            piece = product[line * SIDE : (line + 1) * SIDE, lanes]
            by_col = (piece * col).reshape(SIDE // 8, 8, WIDTH).sum(0)
            by_slope = (piece * col_slope).reshape(SIDE // 8, 8, WIDTH).sum(0)
            row_total = row_total + by_col * row_slopes[line : line + 1]
            col_total = col_total + by_slope * rows[line : line + 1]
        point_grad[row_axis, :, lanes] += row_total
        point_grad[col_axis, :, lanes] += col_total
        return carry

    lax.fori_loop(0, cot.shape[0] // WIDTH, one, 0)

    @pl.when(last_step())
    def _():
        columns = payload[...].T
        rows = columns.shape[1]
        base = 3 * samples
        anchor = [columns[base + c : base + c + 1] for c in range(3)]
        direction = [columns[base + 3 + c : base + 4 + c] for c in range(3)]
        place_grad, way_grad = [], []
        for c in range(3):
            whole = jnp.sum(point_grad[c], axis=0, keepdims=True)
            place = jnp.zeros((1, rows), F32)
            way = jnp.zeros((1, rows), F32)
            for s in range(samples):
                piece = whole[:, s * rows : (s + 1) * rows]
                place = place + piece
                way = way + piece * columns[base + 6 + s : base + 7 + s]
            place_grad.append(place)
            way_grad.append(way)
        turn = []
        for c in range(3):
            d, e = (c + 1) % 3, (c + 2) % 3
            turn.append(
                anchor[d] * place_grad[e]
                - anchor[e] * place_grad[d]
                + direction[d] * way_grad[e]
                - direction[e] * way_grad[d]
            )
        stacked = jnp.concatenate(turn + place_grad + [jnp.zeros((2, rows), F32)], axis=0)
        camera = payload[:, base + 6 + samples : base + 7 + samples]
        cameras = pose_grad.shape[1]
        named = lax.broadcasted_iota(jnp.int32, (rows, cameras), 1).astype(F32) == camera
        pose_grad[...] = exact_dot(stacked, named.astype(F32))


def whole_spec(shape):
    return pl.BlockSpec(shape, lambda *place: (0,) * len(shape))


def shaped(*shape):
    return jax.ShapeDtypeStruct(shape, F32)


def remote_params(number):
    return pltpu.CompilerParams(
        collective_id=number, has_side_effects=True, vmem_limit_bytes=VMEM_BYTES
    )


def per_device(
    anchors,
    directions,
    ray_start,
    camera_ids,
    brick_ids,
    brick_rank,
    targets,
    planes,
    first_weight,
    hidden_weight,
    feature_weight,
    density_weight,
    poses,
):
    count = lax.axis_size(AXES)
    ray_count, segs = brick_ids.shape
    samples = 4
    cap = 2 * ray_count * segs // count
    rows = -(-cap // 8) * 8
    listed = ray_count * segs
    slots = count * cap
    total = slots * samples
    cameras = poses.shape[1]
    in_vmem = pl.BlockSpec(memory_space=pltpu.VMEM)

    per_ray = jnp.concatenate(
        [anchors, directions, ray_start[None], camera_ids.astype(F32)[None]], axis=0
    )
    listing = jnp.concatenate(
        [
            jnp.tile(per_ray, (1, segs)),
            brick_rank.T.reshape(1, listed).astype(F32),
            brick_ids.T.reshape(1, listed).astype(F32),
        ],
        axis=0,
    )

    def narrow(padded):
        if rows == cap:
            return padded
        return padded.reshape(count, rows, -1)[:, :cap].reshape(slots, -1)

    def widen(packed):
        if rows == cap:
            return packed
        grouped = packed.reshape(count, cap, -1)
        return jnp.pad(grouped, ((0, 0), (0, rows - cap), (0, 0))).reshape(count * rows, -1)

    pair = [pltpu.SemaphoreType.DMA((count,)), pltpu.SemaphoreType.DMA((count,))]
    received, route = pl.pallas_call(
        functools.partial(points_kernel, count, rows, samples),
        out_shape=[shaped(count * rows, WIDTH), shaped(count * rows, listed)],
        in_specs=[in_vmem] * 2,
        out_specs=[in_vmem] * 2,
        scratch_shapes=[pltpu.VMEM((count * rows, WIDTH), F32)] * 2 + pair,
        compiler_params=remote_params(0),
        name="send_points",
    )(listing, poses)
    received = narrow(received)

    weights = (first_weight, hidden_weight, feature_weight, density_weight)
    channels = planes.shape[2]
    lines = 16
    cells = lines * SIDE
    grid = (3, SIDE // lines)
    plane_spec = pl.BlockSpec((1, cells, channels), lambda q, i: (0, q * (SIDE // lines) + i, 0))
    local = pltpu.CompilerParams(vmem_limit_bytes=VMEM_BYTES)
    message, features = pl.pallas_call(
        functools.partial(forward_kernel, samples, lines),
        grid=grid,
        out_shape=[shaped(slots, 2 * WIDTH), jax.ShapeDtypeStruct((total, channels), BF16)],
        in_specs=[whole_spec(received.shape), plane_spec]
        + [whole_spec(w.shape) for w in weights],
        out_specs=[whole_spec((slots, 2 * WIDTH)), whole_spec((total, channels))],
        scratch_shapes=[
            pltpu.VMEM((3, SIDE, total), F32),
            pltpu.VMEM((cells, total), BF16),
            pltpu.VMEM((channels, total), F32),
        ],
        compiler_params=local,
        name="brick_forward",
    )(received, planes, *weights)

    wide = (count * rows, 2 * WIDTH)
    ray_feature, incoming = pl.pallas_call(
        functools.partial(owner_kernel, count, rows, ray_count, segs),
        out_shape=[shaped(ray_count, WIDTH), shaped(*wide)],
        in_specs=[in_vmem] * 4,
        out_specs=[in_vmem] * 2,
        scratch_shapes=[pltpu.VMEM(wide, F32)] * 3 + pair + pair,
        compiler_params=remote_params(1),
        name="rays",
    )(widen(message), route, brick_rank, targets)
    incoming = narrow(incoming)

    plane_grad, *weight_grads, pose_local = pl.pallas_call(
        functools.partial(backward_kernel, samples, lines),
        grid=grid,
        out_shape=[
            shaped(*planes.shape),
            *(shaped(*w.shape) for w in weights),
            shaped(8, cameras),
        ],
        in_specs=[whole_spec(received.shape), plane_spec]
        + [whole_spec(w.shape) for w in weights + (features, incoming)],
        out_specs=[plane_spec]
        + [whole_spec(w.shape) for w in weights]
        + [whole_spec((8, cameras))],
        scratch_shapes=[
            pltpu.VMEM((3, SIDE, total), F32),
            pltpu.VMEM((3, SIDE, total), F32),
            pltpu.VMEM((cells, total), BF16),
            pltpu.VMEM((total, channels), BF16),
            pltpu.VMEM((channels, total), BF16),
            pltpu.VMEM((cells, total), F32),
            pltpu.VMEM((3, 8, total), F32),
        ],
        compiler_params=local,
        name="brick_backward",
    )(received, planes, *weights, features, incoming)

    pose_grad = pl.pallas_call(
        functools.partial(pose_kernel, count, 8),
        out_shape=shaped(*poses.shape),
        in_specs=[in_vmem],
        out_specs=in_vmem,
        scratch_shapes=[pltpu.VMEM((count * 8, cameras), F32)] + pair,
        compiler_params=remote_params(2),
        name="sum_poses",
    )(pose_local)
    return (ray_feature, plane_grad, *weight_grads, pose_grad)


def solution(mesh):
    split = P(AXES)
    in_specs = (P(None, AXES), P(None, AXES)) + (split,) * 10 + (P(),)
    out_specs = (split,) * 6 + (P(),)
    return jax.shard_map(
        per_device, mesh=mesh, in_specs=in_specs, out_specs=out_specs, check_vma=False
    )
```

```python
import functools

import jax
import jax.numpy as jnp
from jax import lax
from jax.experimental import pallas as pl
from jax.experimental.pallas import tpu as pltpu
from jax.sharding import PartitionSpec as P

SIDE = 64
STEP = 0.125
WIDTH = 128
AXES = ("gx", "gy")
BF16 = jnp.bfloat16
F32 = jnp.float32
MESH_ID = pl.DeviceIdType.MESH
VMEM_BYTES = 56 * 1024 * 1024


def dot(left, right, left_dim=1, right_dim=0, precision=None):
    return lax.dot_general(
        left,
        right,
        (((left_dim,), (right_dim,)), ((), ())),
        precision=precision,
        preferred_element_type=F32,
    )


def exact_dot(left, right, left_dim=1, right_dim=0):
    return dot(left, right, left_dim, right_dim, lax.Precision.HIGHEST)


def peer_id(index):
    side = lax.axis_size("gy")
    return (index // side, index % side)


def my_index():
    return lax.axis_index("gx") * lax.axis_size("gy") + lax.axis_index("gy")


def enter(count):
    me = my_index()
    barrier = pltpu.get_barrier_semaphore()

    def greet(step, carry):
        pl.semaphore_signal(
            barrier, inc=1, device_id=peer_id((me + step) % count), device_id_type=MESH_ID
        )
        return carry

    lax.fori_loop(1, count, greet, 0)


def all_entered(count):
    pl.semaphore_wait(pltpu.get_barrier_semaphore(), count - 1)


def rows_of(ref, index, rows):
    return ref.at[pl.ds(pl.multiple_of(index * rows, 8), rows)]


def remote_copy(count, step, source, target, rows, send_sem, recv_sem):
    me = my_index()
    peer = (me + step) % count
    return pltpu.make_async_remote_copy(
        src_ref=rows_of(source, peer, rows),
        dst_ref=rows_of(target, me, rows),
        send_sem=send_sem.at[step],
        recv_sem=recv_sem.at[me],
        device_id=peer_id(peer),
        device_id_type=MESH_ID,
    )


def send_all(count, source, target, rows, send_sem, recv_sem):
    def send(step, carry):
        remote_copy(count, step, source, target, rows, send_sem, recv_sem).start()
        return carry

    lax.fori_loop(1, count, send, 0)


def wait_all(count, source, target, rows, send_sem, recv_sem):
    me = my_index()

    def arrive(step, carry):
        origin = (me + count - step) % count
        pltpu.make_async_remote_copy(
            src_ref=rows_of(source, origin, rows),
            dst_ref=rows_of(target, origin, rows),
            send_sem=send_sem.at[step],
            recv_sem=recv_sem.at[origin],
            device_id=peer_id(origin),
            device_id_type=MESH_ID,
        ).wait_recv()
        return carry

    lax.fori_loop(1, count, arrive, 0)

    def leave(step, carry):
        remote_copy(count, step, source, target, rows, send_sem, recv_sem).wait_send()
        return carry

    lax.fori_loop(1, count, leave, 0)


def keep_own(source, target, rows):
    here = pl.ds(pl.multiple_of(my_index() * rows, 8), rows)
    target[here, :] = source[here, :]


def cross_rows(left, right):
    return [
        left[1] * right[2] - left[2] * right[1],
        left[2] * right[0] - left[0] * right[2],
        left[0] * right[1] - left[1] * right[0],
    ]


def row_list(array, start, number):
    return [array[start + c : start + c + 1] for c in range(number)]


def points_kernel(
    count, rows, samples, listing, poses, received, route_out, sent, landed, send_sem, recv_sem
):
    enter(count)
    listed = listing.shape[1]
    anchors = row_list(listing, 0, 3)
    directions = row_list(listing, 3, 3)
    ray_start, camera, rank, brick = row_list(listing, 6, 4)
    cameras = lax.broadcasted_iota(jnp.int32, (poses.shape[1], listed), 0).astype(F32)
    ray_pose = exact_dot(poses[...], (cameras == camera).astype(F32))
    turned_anchor = cross_rows(row_list(ray_pose, 0, 3), anchors)
    turned_direction = cross_rows(row_list(ray_pose, 0, 3), directions)
    moved_anchor = [anchors[c] + turned_anchor[c] + ray_pose[3 + c : 4 + c] for c in range(3)]
    moved_direction = [directions[c] + turned_direction[c] for c in range(3)]
    distance = [ray_start + (rank * samples + s + 0.5) * STEP for s in range(samples)]
    payload = [
        moved_anchor[c] + distance[s] * moved_direction[c]
        for c in range(3)
        for s in range(samples)
    ]
    payload = payload + anchors + directions + distance + [camera]
    filler = jnp.zeros((WIDTH - len(payload), listed), F32)
    payload = jnp.concatenate(payload + [filler], axis=0)
    bricks = lax.broadcasted_iota(jnp.int32, (count, listed), 0).astype(F32)
    named = (bricks == brick).astype(F32)
    earlier = lax.broadcasted_iota(jnp.int32, (listed, listed), 0)
    later = lax.broadcasted_iota(jnp.int32, (listed, listed), 1)
    before = dot(named.astype(BF16), (earlier < later).astype(BF16))
    slot = brick * rows + jnp.sum(before * named, axis=0, keepdims=True)
    slots = lax.broadcasted_iota(jnp.int32, (count * rows, listed), 0).astype(F32)
    route = (slots == slot).astype(F32)
    route_out[...] = route
    sent[...] = exact_dot(route, payload, 1, 1)
    all_entered(count)
    send_all(count, sent, landed, rows, send_sem, recv_sem)
    keep_own(sent, landed, rows)
    wait_all(count, sent, landed, rows, send_sem, recv_sem)
    received[...] = landed[...]


def owner_kernel(
    count,
    rows,
    ray_count,
    segs,
    sent,
    route,
    listing,
    targets,
    ray_out,
    received,
    home,
    outgoing,
    landed,
    send_sem,
    recv_sem,
    send_sem2,
    recv_sem2,
):
    enter(count)
    all_entered(count)
    send_all(count, sent, home, rows, send_sem, recv_sem)
    keep_own(sent, home, rows)
    wait_all(count, sent, home, rows, send_sem, recv_sem)
    listed = exact_dot(route[...], home[...], 0, 0)
    feature = [listed[k * ray_count : (k + 1) * ray_count, :WIDTH] for k in range(segs)]
    passing = [listed[k * ray_count : (k + 1) * ray_count, WIDTH:] for k in range(segs)]
    ranks = jnp.broadcast_to(listing[8:9, :], (WIDTH, segs * ray_count)).T
    rank = [ranks[k * ray_count : (k + 1) * ray_count] for k in range(segs)]

    def through(k, skipped):
        product = jnp.ones((ray_count, WIDTH), F32)
        for other in range(segs):
            if other != k and other != skipped:
                product = product * jnp.where(rank[other] < rank[k], passing[other], 1.0)
        return product

    transmit = [through(k, k) for k in range(segs)]
    ray = transmit[0] * feature[0]
    for k in range(1, segs):
        ray = ray + transmit[k] * feature[k]
    ray_out[...] = ray
    residual = ray - targets[...]
    along = [jnp.sum(residual * feature[k], axis=1, keepdims=True) for k in range(segs)]
    back = []
    for k in range(segs):
        pass_grad = jnp.zeros((ray_count, WIDTH), F32)
        for behind in range(segs):
            if behind != k:
                pass_grad = pass_grad + jnp.where(
                    rank[k] < rank[behind], through(behind, k) * along[behind], 0.0
                )
        back.append(jnp.concatenate([transmit[k] * residual, pass_grad], axis=1))
    outgoing[...] = exact_dot(route[...], jnp.concatenate(back, axis=0))
    send_all(count, outgoing, landed, rows, send_sem2, recv_sem2)
    keep_own(outgoing, landed, rows)
    wait_all(count, outgoing, landed, rows, send_sem2, recv_sem2)
    received[...] = landed[...]


def along_axis(axis, index):
    place = {name: lax.axis_index(name) for name in AXES}
    place[axis] = index
    return tuple(place[name] for name in AXES)


def share_along(axis, rows, own, landed, send_sem, recv_sem):
    count, me = lax.axis_size(axis), lax.axis_index(axis)

    def copy(step, target, index):
        return pltpu.make_async_remote_copy(
            src_ref=own,
            dst_ref=rows_of(landed, index, rows),
            send_sem=send_sem.at[step],
            recv_sem=recv_sem.at[index],
            device_id=along_axis(axis, target),
            device_id_type=MESH_ID,
        )

    for step in range(1, count):
        copy(step, (me + step) % count, me).start()
    landed[pl.ds(pl.multiple_of(me * rows, 8), rows), :] = own[...]
    for step in range(1, count):
        origin = (me + count - step) % count
        copy(step, origin, origin).wait_recv()
    for step in range(1, count):
        copy(step, (me + step) % count, me).wait_send()
    summed = landed[0:rows, :]
    for index in range(1, count):
        summed = summed + landed[index * rows : (index + 1) * rows, :]
    return summed


def pose_kernel(rows, own, total, near, part, far, near_send, near_recv, far_send, far_recv):
    barrier = pltpu.get_barrier_semaphore()
    greeted = 0
    for axis in AXES:
        count = lax.axis_size(axis)
        for step in range(1, count):
            pl.semaphore_signal(
                barrier,
                inc=1,
                device_id=along_axis(axis, (lax.axis_index(axis) + step) % count),
                device_id_type=MESH_ID,
            )
        greeted += count - 1
    pl.semaphore_wait(barrier, greeted)
    part[...] = share_along("gy", rows, own, near, near_send, near_recv)
    summed = share_along("gx", rows, part, far, far_send, far_recv)
    total[...] = summed[: total.shape[0]]


def coordinate_rows(payload, samples):
    columns = payload.T
    return [
        jnp.concatenate([columns[c * samples + s : c * samples + s + 1] for s in range(samples)], 1)
        for c in range(3)
    ]


def fill_factors(coords, factor, slope=None):
    total = coords[0].shape[1]
    cells = lax.broadcasted_iota(jnp.int32, (SIDE, total), 0)
    for c in range(3):
        scaled = coords[c] * float(SIDE)
        floor_c = jnp.floor(scaled)
        fraction = scaled - floor_c
        weight = fraction * fraction * (3.0 - 2.0 * fraction)
        low = floor_c.astype(jnp.int32) & (SIDE - 1)
        high = (low + 1) & (SIDE - 1)
        low_hit = cells == low
        high_hit = cells == high
        factor[c] = jnp.where(low_hit, 1.0 - weight, jnp.where(high_hit, weight, 0.0))
        if slope is not None:
            change = float(SIDE) * 6.0 * fraction * (1.0 - fraction)
            slope[c] = jnp.where(low_hit, -change, jnp.where(high_hit, change, 0.0))


def block_place(lines):
    plane, block = pl.program_id(0), pl.program_id(1)
    return plane // 2, (plane + 3) // 2, block * lines


def fill_table(factor, table, lines):
    row_axis, col_axis, first = block_place(lines)
    rows = factor[row_axis, pl.ds(pl.multiple_of(first, 8), lines), :]
    for line in range(lines):
        table[line * SIDE : (line + 1) * SIDE, :] = (
            rows[line : line + 1] * factor[col_axis]
        ).astype(BF16)


def bf16_weights(first, hidden, feature, density):
    column = jnp.broadcast_to(density[...], (WIDTH, density.shape[1])).T
    heads = jnp.concatenate([feature[0], column], axis=1).astype(BF16)
    return first[0].astype(BF16), hidden[0, 0].astype(BF16), heads


def network(features, first, hidden, heads):
    pre1 = dot(features, first)
    gate1 = jax.nn.sigmoid(pre1)
    hidden1 = (pre1 * gate1).astype(BF16)
    pre2 = dot(hidden1, hidden)
    gate2 = jax.nn.sigmoid(pre2)
    hidden2 = (pre2 * gate2).astype(BF16)
    last = dot(hidden2, heads)
    colors = jnp.tanh(last[:, :WIDTH])
    raw = last[:, WIDTH:]
    density = jnp.maximum(raw, 0.0) + jnp.log1p(jnp.exp(-jnp.abs(raw)))
    return pre1, gate1, hidden1, pre2, gate2, hidden2, colors, raw, density


def transmittance(density, samples):
    rows = density.shape[0] // samples
    depth = [density[s * rows : (s + 1) * rows] * STEP for s in range(samples)]
    before = jnp.zeros_like(depth[0])
    reach, kept = [], []
    for s in range(samples):
        reach.append(jnp.exp(-before))
        kept.append(jnp.exp(-depth[s]))
        before = before + depth[s]
    return reach, kept, jnp.exp(-before)


def last_step():
    return (pl.program_id(0) == pl.num_programs(0) - 1) & (
        pl.program_id(1) == pl.num_programs(1) - 1
    )


def first_step():
    return (pl.program_id(0) == 0) & (pl.program_id(1) == 0)


def forward_kernel(
    samples,
    lines,
    payload,
    planes,
    first,
    hidden,
    feature,
    density,
    message,
    features,
    factor,
    table,
    summed,
):
    @pl.when(first_step())
    def _():
        fill_factors(coordinate_rows(payload[...], samples), factor)
        summed[...] = jnp.zeros_like(summed)

    fill_table(factor, table, lines)
    summed[...] += dot(planes[0].T.astype(BF16), table[...])

    @pl.when(last_step())
    def _():
        rounded = summed[...].T.astype(BF16)
        features[...] = rounded
        parts = network(rounded, *bf16_weights(first, hidden, feature, density))
        colors = parts[6]
        reach, kept, passing = transmittance(parts[8], samples)
        rows = passing.shape[0]
        value = jnp.zeros_like(passing)
        for s in range(samples):
            value = value + reach[s] * (1.0 - kept[s]) * colors[s * rows : (s + 1) * rows]
        message[:, :WIDTH] = value
        message[:, WIDTH:] = passing


def silu_slope(pre, gate):
    return gate * (1.0 + pre * (1.0 - gate))


def backward_kernel(
    samples,
    lines,
    payload,
    planes,
    first,
    hidden,
    feature,
    density,
    features,
    incoming,
    plane_grad,
    first_grad,
    hidden_grad,
    feature_grad,
    density_grad,
    pose_grad,
    factor,
    slope,
    table,
    cot,
    cot_rows,
    product,
    point_grad,
):
    @pl.when(first_step())
    def _():
        fill_factors(coordinate_rows(payload[...], samples), factor, slope)
        point_grad[...] = jnp.zeros_like(point_grad)
        weight1, weight2, heads = bf16_weights(first, hidden, feature, density)
        pre1, gate1, hidden1, pre2, gate2, hidden2, colors, raw, thick = network(
            features[...], weight1, weight2, heads
        )
        reach, kept, passing = transmittance(thick, samples)
        rows = passing.shape[0]
        feature_cot = incoming[:, :WIDTH]
        pass_cot = incoming[:, WIDTH:] * passing
        behind = pass_cot
        color_cots = [None] * samples
        depth_cots = [None] * samples
        for s in reversed(range(samples)):
            here = colors[s * rows : (s + 1) * rows]
            along = jnp.sum(feature_cot * here, axis=1, keepdims=True)
            weight = reach[s] * (1.0 - kept[s])
            color_cots[s] = weight * feature_cot * (1.0 - here * here)
            depth_cots[s] = along * reach[s] * kept[s] - behind
            behind = behind + along * weight
        raw_cot = jnp.concatenate(depth_cots, axis=0) * STEP * jax.nn.sigmoid(raw)
        lane = lax.broadcasted_iota(jnp.int32, raw_cot.shape, 1)
        raw_cot = jnp.where(lane == 0, raw_cot, 0.0)
        last_cot = jnp.concatenate([jnp.concatenate(color_cots, axis=0), raw_cot], axis=1)
        last_cot = last_cot.astype(BF16)
        feature_grad[0] = dot(hidden2, last_cot[:, :WIDTH], 0, 0).astype(BF16).astype(F32)
        by_density = dot(last_cot[:, WIDTH:], hidden2, 0, 0)
        density_grad[...] = by_density[0:1].astype(BF16).astype(F32)
        cot2 = dot(last_cot, heads, 1, 1).astype(BF16).astype(F32)
        cot2 = (cot2 * silu_slope(pre2, gate2)).astype(BF16)
        hidden_grad[0, 0] = dot(hidden1, cot2, 0, 0).astype(BF16).astype(F32)
        cot1 = dot(cot2, weight2, 1, 1).astype(BF16).astype(F32)
        cot1 = (cot1 * silu_slope(pre1, gate1)).astype(BF16)
        first_grad[0] = dot(features[...], cot1, 0, 0).astype(BF16).astype(F32)
        sample_cot = dot(cot1, weight1, 1, 1)
        cot[...] = sample_cot.astype(BF16)
        cot_rows[...] = sample_cot.T.astype(BF16)

    product[...] = dot(planes[0].astype(BF16), cot_rows[...])
    fill_table(factor, table, lines)
    plane_grad[0] = dot(table[...], cot[...])
    row_axis, col_axis, first_line = block_place(lines)

    def one(chunk, carry):
        lanes = pl.ds(pl.multiple_of(chunk * WIDTH, WIDTH), WIDTH)
        col, col_slope = factor[col_axis, :, lanes], slope[col_axis, :, lanes]
        here = pl.ds(pl.multiple_of(first_line, 8), lines)
        rows, row_slopes = factor[row_axis, here, lanes], slope[row_axis, here, lanes]
        row_total = jnp.zeros((8, WIDTH), F32)
        col_total = jnp.zeros((8, WIDTH), F32)
        for line in range(lines):
            piece = product[line * SIDE : (line + 1) * SIDE, lanes]
            by_col = (piece * col).reshape(SIDE // 8, 8, WIDTH).sum(0)
            by_slope = (piece * col_slope).reshape(SIDE // 8, 8, WIDTH).sum(0)
            row_total = row_total + by_col * row_slopes[line : line + 1]
            col_total = col_total + by_slope * rows[line : line + 1]
        point_grad[row_axis, :, lanes] += row_total
        point_grad[col_axis, :, lanes] += col_total
        return carry

    lax.fori_loop(0, cot.shape[0] // WIDTH, one, 0, unroll=True)

    @pl.when(last_step())
    def _():
        columns = payload[...].T
        rows = columns.shape[1]
        base = 3 * samples
        anchor = [columns[base + c : base + c + 1] for c in range(3)]
        direction = [columns[base + 3 + c : base + 4 + c] for c in range(3)]
        place_grad, way_grad = [], []
        for c in range(3):
            whole = jnp.sum(point_grad[c], axis=0, keepdims=True)
            place = jnp.zeros((1, rows), F32)
            way = jnp.zeros((1, rows), F32)
            for s in range(samples):
                piece = whole[:, s * rows : (s + 1) * rows]
                place = place + piece
                way = way + piece * columns[base + 6 + s : base + 7 + s]
            place_grad.append(place)
            way_grad.append(way)
        turn = []
        for c in range(3):
            d, e = (c + 1) % 3, (c + 2) % 3
            turn.append(
                anchor[d] * place_grad[e]
                - anchor[e] * place_grad[d]
                + direction[d] * way_grad[e]
                - direction[e] * way_grad[d]
            )
        stacked = jnp.concatenate(turn + place_grad + [jnp.zeros((2, rows), F32)], axis=0)
        camera = payload[:, base + 6 + samples : base + 7 + samples]
        cameras = pose_grad.shape[1]
        named = lax.broadcasted_iota(jnp.int32, (rows, cameras), 1).astype(F32) == camera
        pose_grad[...] = exact_dot(stacked, named.astype(F32))


def whole_spec(shape):
    return pl.BlockSpec(shape, lambda *place: (0,) * len(shape))


def shaped(*shape):
    return jax.ShapeDtypeStruct(shape, F32)


def remote_params(number):
    return pltpu.CompilerParams(
        collective_id=number, has_side_effects=True, vmem_limit_bytes=VMEM_BYTES
    )


def per_device(
    anchors,
    directions,
    ray_start,
    camera_ids,
    brick_ids,
    brick_rank,
    targets,
    planes,
    first_weight,
    hidden_weight,
    feature_weight,
    density_weight,
    poses,
):
    count = lax.axis_size(AXES)
    ray_count, segs = brick_ids.shape
    samples = 4
    cap = 2 * ray_count * segs // count
    rows = -(-cap // 8) * 8
    listed = ray_count * segs
    slots = count * cap
    total = slots * samples
    cameras = poses.shape[1]
    in_vmem = pl.BlockSpec(memory_space=pltpu.VMEM)

    per_ray = jnp.concatenate(
        [anchors, directions, ray_start[None], camera_ids.astype(F32)[None]], axis=0
    )
    listing = jnp.concatenate(
        [
            jnp.tile(per_ray, (1, segs)),
            brick_rank.T.reshape(1, listed).astype(F32),
            brick_ids.T.reshape(1, listed).astype(F32),
        ],
        axis=0,
    )

    def narrow(padded):
        if rows == cap:
            return padded
        return padded.reshape(count, rows, -1)[:, :cap].reshape(slots, -1)

    def widen(packed):
        if rows == cap:
            return packed
        grouped = packed.reshape(count, cap, -1)
        return jnp.pad(grouped, ((0, 0), (0, rows - cap), (0, 0))).reshape(count * rows, -1)

    pair = [pltpu.SemaphoreType.DMA((count,)), pltpu.SemaphoreType.DMA((count,))]
    received, route = pl.pallas_call(
        functools.partial(points_kernel, count, rows, samples),
        out_shape=[shaped(count * rows, WIDTH), shaped(count * rows, listed)],
        in_specs=[in_vmem] * 2,
        out_specs=[in_vmem] * 2,
        scratch_shapes=[pltpu.VMEM((count * rows, WIDTH), F32)] * 2 + pair,
        compiler_params=remote_params(0),
        name="send_points",
    )(listing, poses)
    received = narrow(received)

    weights = (first_weight, hidden_weight, feature_weight, density_weight)
    channels = planes.shape[2]
    lines = 16
    cells = lines * SIDE
    grid = (3, SIDE // lines)
    plane_spec = pl.BlockSpec((1, cells, channels), lambda q, i: (0, q * (SIDE // lines) + i, 0))
    local = pltpu.CompilerParams(vmem_limit_bytes=VMEM_BYTES)
    message, features = pl.pallas_call(
        functools.partial(forward_kernel, samples, lines),
        grid=grid,
        out_shape=[shaped(slots, 2 * WIDTH), jax.ShapeDtypeStruct((total, channels), BF16)],
        in_specs=[whole_spec(received.shape), plane_spec]
        + [whole_spec(w.shape) for w in weights],
        out_specs=[whole_spec((slots, 2 * WIDTH)), whole_spec((total, channels))],
        scratch_shapes=[
            pltpu.VMEM((3, SIDE, total), F32),
            pltpu.VMEM((cells, total), BF16),
            pltpu.VMEM((channels, total), F32),
        ],
        compiler_params=local,
        name="brick_forward",
    )(received, planes, *weights)

    wide = (count * rows, 2 * WIDTH)
    ray_feature, incoming = pl.pallas_call(
        functools.partial(owner_kernel, count, rows, ray_count, segs),
        out_shape=[shaped(ray_count, WIDTH), shaped(*wide)],
        in_specs=[in_vmem] * 4,
        out_specs=[in_vmem] * 2,
        scratch_shapes=[pltpu.VMEM(wide, F32)] * 3 + pair + pair,
        compiler_params=remote_params(1),
        name="rays",
    )(widen(message), route, listing, targets)
    incoming = narrow(incoming)

    plane_grad, *weight_grads, pose_local = pl.pallas_call(
        functools.partial(backward_kernel, samples, lines),
        grid=grid,
        out_shape=[
            shaped(*planes.shape),
            *(shaped(*w.shape) for w in weights),
            shaped(8, cameras),
        ],
        in_specs=[whole_spec(received.shape), plane_spec]
        + [whole_spec(w.shape) for w in weights + (features, incoming)],
        out_specs=[plane_spec]
        + [whole_spec(w.shape) for w in weights]
        + [whole_spec((8, cameras))],
        scratch_shapes=[
            pltpu.VMEM((3, SIDE, total), F32),
            pltpu.VMEM((3, SIDE, total), F32),
            pltpu.VMEM((cells, total), BF16),
            pltpu.VMEM((total, channels), BF16),
            pltpu.VMEM((channels, total), BF16),
            pltpu.VMEM((cells, total), F32),
            pltpu.VMEM((3, 8, total), F32),
        ],
        compiler_params=local,
        name="brick_backward",
    )(received, planes, *weights, features, incoming)

    far, near = (lax.axis_size(axis) for axis in AXES)
    pose_grad = pl.pallas_call(
        functools.partial(pose_kernel, 8),
        out_shape=shaped(*poses.shape),
        in_specs=[in_vmem],
        out_specs=in_vmem,
        scratch_shapes=[
            pltpu.VMEM((8 * near, cameras), F32),
            pltpu.VMEM((8, cameras), F32),
            pltpu.VMEM((8 * far, cameras), F32),
        ]
        + [pltpu.SemaphoreType.DMA((near,))] * 2
        + [pltpu.SemaphoreType.DMA((far,))] * 2,
        compiler_params=remote_params(2),
        name="sum_poses",
    )(pose_local)
    return (ray_feature, plane_grad, *weight_grads, pose_grad)


def solution(mesh):
    split = P(AXES)
    in_specs = (P(None, AXES), P(None, AXES)) + (split,) * 10 + (P(),)
    out_specs = (split,) * 6 + (P(),)
    return jax.shard_map(
        per_device, mesh=mesh, in_specs=in_specs, out_specs=out_specs, check_vma=False
    )
```

```python
import functools

import jax
import jax.numpy as jnp
from jax import lax
from jax.experimental import pallas as pl
from jax.experimental.pallas import tpu as pltpu
from jax.sharding import PartitionSpec as P

SIDE = 64
STEP = 0.125
WIDTH = 128
AXES = ("gx", "gy")
BF16 = jnp.bfloat16
F32 = jnp.float32
MESH_ID = pl.DeviceIdType.MESH
VMEM_BYTES = 56 * 1024 * 1024


def dot(left, right, left_dim=1, right_dim=0, precision=None):
    return lax.dot_general(
        left,
        right,
        (((left_dim,), (right_dim,)), ((), ())),
        precision=precision,
        preferred_element_type=F32,
    )


def exact_dot(left, right, left_dim=1, right_dim=0):
    return dot(left, right, left_dim, right_dim, lax.Precision.HIGHEST)


def peer_id(index):
    side = lax.axis_size("gy")
    return (index // side, index % side)


def my_index():
    return lax.axis_index("gx") * lax.axis_size("gy") + lax.axis_index("gy")


def enter(count):
    me = my_index()
    barrier = pltpu.get_barrier_semaphore()

    def greet(step, carry):
        pl.semaphore_signal(
            barrier, inc=1, device_id=peer_id((me + step) % count), device_id_type=MESH_ID
        )
        return carry

    lax.fori_loop(1, count, greet, 0)


def all_entered(count):
    pl.semaphore_wait(pltpu.get_barrier_semaphore(), count - 1)


def rows_of(ref, index, rows):
    return ref.at[pl.ds(pl.multiple_of(index * rows, 8), rows)]


def remote_copy(count, step, source, target, rows, send_sem, recv_sem):
    me = my_index()
    peer = (me + step) % count
    return pltpu.make_async_remote_copy(
        src_ref=rows_of(source, peer, rows),
        dst_ref=rows_of(target, me, rows),
        send_sem=send_sem.at[step],
        recv_sem=recv_sem.at[me],
        device_id=peer_id(peer),
        device_id_type=MESH_ID,
    )


def send_all(count, source, target, rows, send_sem, recv_sem):
    def send(step, carry):
        remote_copy(count, step, source, target, rows, send_sem, recv_sem).start()
        return carry

    lax.fori_loop(1, count, send, 0)


def wait_all(count, source, target, rows, send_sem, recv_sem):
    me = my_index()

    def arrive(step, carry):
        origin = (me + count - step) % count
        pltpu.make_async_remote_copy(
            src_ref=rows_of(source, origin, rows),
            dst_ref=rows_of(target, origin, rows),
            send_sem=send_sem.at[step],
            recv_sem=recv_sem.at[origin],
            device_id=peer_id(origin),
            device_id_type=MESH_ID,
        ).wait_recv()
        return carry

    lax.fori_loop(1, count, arrive, 0)

    def leave(step, carry):
        remote_copy(count, step, source, target, rows, send_sem, recv_sem).wait_send()
        return carry

    lax.fori_loop(1, count, leave, 0)


def keep_own(source, target, rows):
    here = pl.ds(pl.multiple_of(my_index() * rows, 8), rows)
    target[here, :] = source[here, :]


def cross_rows(left, right):
    return [
        left[1] * right[2] - left[2] * right[1],
        left[2] * right[0] - left[0] * right[2],
        left[0] * right[1] - left[1] * right[0],
    ]


def row_list(array, start, number):
    return [array[start + c : start + c + 1] for c in range(number)]


def points_kernel(
    count, rows, samples, listing, poses, received, route_out, sent, landed, send_sem, recv_sem
):
    enter(count)
    listed = listing.shape[1]
    anchors = row_list(listing, 0, 3)
    directions = row_list(listing, 3, 3)
    ray_start, camera, rank, brick = row_list(listing, 6, 4)
    cameras = lax.broadcasted_iota(jnp.int32, (poses.shape[1], listed), 0).astype(F32)
    ray_pose = exact_dot(poses[...], (cameras == camera).astype(F32))
    turned_anchor = cross_rows(row_list(ray_pose, 0, 3), anchors)
    turned_direction = cross_rows(row_list(ray_pose, 0, 3), directions)
    moved_anchor = [anchors[c] + turned_anchor[c] + ray_pose[3 + c : 4 + c] for c in range(3)]
    moved_direction = [directions[c] + turned_direction[c] for c in range(3)]
    distance = [ray_start + (rank * samples + s + 0.5) * STEP for s in range(samples)]
    payload = [
        moved_anchor[c] + distance[s] * moved_direction[c]
        for c in range(3)
        for s in range(samples)
    ]
    payload = payload + anchors + directions + distance + [camera]
    filler = jnp.zeros((WIDTH - len(payload), listed), F32)
    payload = jnp.concatenate(payload + [filler], axis=0)
    bricks = lax.broadcasted_iota(jnp.int32, (count, listed), 0).astype(F32)
    named = (bricks == brick).astype(F32)
    earlier = lax.broadcasted_iota(jnp.int32, (listed, listed), 0)
    later = lax.broadcasted_iota(jnp.int32, (listed, listed), 1)
    before = dot(named.astype(BF16), (earlier < later).astype(BF16))
    slot = brick * rows + jnp.sum(before * named, axis=0, keepdims=True)
    slots = lax.broadcasted_iota(jnp.int32, (count * rows, listed), 0).astype(F32)
    route = (slots == slot).astype(F32)
    route_out[...] = route
    sent[...] = exact_dot(route, payload, 1, 1)
    all_entered(count)
    send_all(count, sent, landed, rows, send_sem, recv_sem)
    keep_own(sent, landed, rows)
    wait_all(count, sent, landed, rows, send_sem, recv_sem)
    received[...] = landed[...]


def owner_kernel(
    count,
    rows,
    ray_count,
    segs,
    sent,
    route,
    listing,
    targets,
    ray_out,
    received,
    home,
    outgoing,
    landed,
    send_sem,
    recv_sem,
    send_sem2,
    recv_sem2,
    greeted=False,
):
    if not greeted:
        enter(count)
    all_entered(count)
    send_all(count, sent, home, rows, send_sem, recv_sem)
    keep_own(sent, home, rows)
    wait_all(count, sent, home, rows, send_sem, recv_sem)
    listed = exact_dot(route[...], home[...], 0, 0)
    feature = [listed[k * ray_count : (k + 1) * ray_count, :WIDTH] for k in range(segs)]
    passing = [listed[k * ray_count : (k + 1) * ray_count, WIDTH:] for k in range(segs)]
    ranks = jnp.broadcast_to(listing[8:9, :], (WIDTH, segs * ray_count)).T
    rank = [ranks[k * ray_count : (k + 1) * ray_count] for k in range(segs)]

    def through(k, skipped):
        product = jnp.ones((ray_count, WIDTH), F32)
        for other in range(segs):
            if other != k and other != skipped:
                product = product * jnp.where(rank[other] < rank[k], passing[other], 1.0)
        return product

    transmit = [through(k, k) for k in range(segs)]
    ray = transmit[0] * feature[0]
    for k in range(1, segs):
        ray = ray + transmit[k] * feature[k]
    ray_out[...] = ray
    residual = ray - targets[...]
    along = [jnp.sum(residual * feature[k], axis=1, keepdims=True) for k in range(segs)]
    back = []
    for k in range(segs):
        pass_grad = jnp.zeros((ray_count, WIDTH), F32)
        for behind in range(segs):
            if behind != k:
                pass_grad = pass_grad + jnp.where(
                    rank[k] < rank[behind], through(behind, k) * along[behind], 0.0
                )
        back.append(jnp.concatenate([transmit[k] * residual, pass_grad], axis=1))
    outgoing[...] = exact_dot(route[...], jnp.concatenate(back, axis=0))
    send_all(count, outgoing, landed, rows, send_sem2, recv_sem2)
    keep_own(outgoing, landed, rows)
    wait_all(count, outgoing, landed, rows, send_sem2, recv_sem2)
    received[...] = landed[...]


def along_axis(axis, index):
    place = {name: lax.axis_index(name) for name in AXES}
    place[axis] = index
    return tuple(place[name] for name in AXES)


def share_along(axis, rows, own, landed, send_sem, recv_sem):
    count, me = lax.axis_size(axis), lax.axis_index(axis)

    def copy(step, target, index):
        return pltpu.make_async_remote_copy(
            src_ref=own,
            dst_ref=rows_of(landed, index, rows),
            send_sem=send_sem.at[step],
            recv_sem=recv_sem.at[index],
            device_id=along_axis(axis, target),
            device_id_type=MESH_ID,
        )

    for step in range(1, count):
        copy(step, (me + step) % count, me).start()
    landed[pl.ds(pl.multiple_of(me * rows, 8), rows), :] = own[...]
    for step in range(1, count):
        origin = (me + count - step) % count
        copy(step, origin, origin).wait_recv()
    for step in range(1, count):
        copy(step, (me + step) % count, me).wait_send()
    summed = landed[0:rows, :]
    for index in range(1, count):
        summed = summed + landed[index * rows : (index + 1) * rows, :]
    return summed


def pose_kernel(rows, own, total, near, part, far, near_send, near_recv, far_send, far_recv):
    barrier = pltpu.get_barrier_semaphore()
    greeted = 0
    for axis in AXES:
        count = lax.axis_size(axis)
        for step in range(1, count):
            pl.semaphore_signal(
                barrier,
                inc=1,
                device_id=along_axis(axis, (lax.axis_index(axis) + step) % count),
                device_id_type=MESH_ID,
            )
        greeted += count - 1
    pl.semaphore_wait(barrier, greeted)
    part[...] = share_along("gy", rows, own, near, near_send, near_recv)
    summed = share_along("gx", rows, part, far, far_send, far_recv)
    total[...] = summed[: total.shape[0]]


def coordinate_rows(payload, samples):
    columns = payload.T
    return [
        jnp.concatenate([columns[c * samples + s : c * samples + s + 1] for s in range(samples)], 1)
        for c in range(3)
    ]


def fill_factors(coords, factor, slope=None):
    total = coords[0].shape[1]
    cells = lax.broadcasted_iota(jnp.int32, (SIDE, total), 0)
    for c in range(3):
        scaled = coords[c] * float(SIDE)
        floor_c = jnp.floor(scaled)
        fraction = scaled - floor_c
        weight = fraction * fraction * (3.0 - 2.0 * fraction)
        low = floor_c.astype(jnp.int32) & (SIDE - 1)
        high = (low + 1) & (SIDE - 1)
        low_hit = cells == low
        high_hit = cells == high
        factor[c] = jnp.where(low_hit, 1.0 - weight, jnp.where(high_hit, weight, 0.0))
        if slope is not None:
            change = float(SIDE) * 6.0 * fraction * (1.0 - fraction)
            slope[c] = jnp.where(low_hit, -change, jnp.where(high_hit, change, 0.0))


def block_place(lines):
    plane, block = pl.program_id(0), pl.program_id(1)
    return plane // 2, (plane + 3) // 2, block * lines


def fill_table(factor, table, lines):
    row_axis, col_axis, first = block_place(lines)
    rows = factor[row_axis, pl.ds(pl.multiple_of(first, 8), lines), :]
    for line in range(lines):
        table[line * SIDE : (line + 1) * SIDE, :] = (
            rows[line : line + 1] * factor[col_axis]
        ).astype(BF16)


def bf16_weights(first, hidden, feature, density):
    column = jnp.broadcast_to(density[...], (WIDTH, density.shape[1])).T
    heads = jnp.concatenate([feature[0], column], axis=1).astype(BF16)
    return first[0].astype(BF16), hidden[0, 0].astype(BF16), heads


def network(features, first, hidden, heads):
    pre1 = dot(features, first)
    gate1 = jax.nn.sigmoid(pre1)
    hidden1 = (pre1 * gate1).astype(BF16)
    pre2 = dot(hidden1, hidden)
    gate2 = jax.nn.sigmoid(pre2)
    hidden2 = (pre2 * gate2).astype(BF16)
    last = dot(hidden2, heads)
    colors = jnp.tanh(last[:, :WIDTH])
    raw = last[:, WIDTH:]
    density = jnp.maximum(raw, 0.0) + jnp.log1p(jnp.exp(-jnp.abs(raw)))
    return pre1, gate1, hidden1, pre2, gate2, hidden2, colors, raw, density


def transmittance(density, samples):
    rows = density.shape[0] // samples
    depth = [density[s * rows : (s + 1) * rows] * STEP for s in range(samples)]
    before = jnp.zeros_like(depth[0])
    reach, kept = [], []
    for s in range(samples):
        reach.append(jnp.exp(-before))
        kept.append(jnp.exp(-depth[s]))
        before = before + depth[s]
    return reach, kept, jnp.exp(-before)


def last_step():
    return (pl.program_id(0) == pl.num_programs(0) - 1) & (
        pl.program_id(1) == pl.num_programs(1) - 1
    )


def first_step():
    return (pl.program_id(0) == 0) & (pl.program_id(1) == 0)


def forward_kernel(
    samples,
    lines,
    payload,
    planes,
    first,
    hidden,
    feature,
    density,
    message,
    features,
    factor,
    table,
    summed,
):
    @pl.when(first_step())
    def _():
        fill_factors(coordinate_rows(payload[...], samples), factor)
        summed[...] = jnp.zeros_like(summed)

    fill_table(factor, table, lines)
    summed[...] += dot(planes[0].T.astype(BF16), table[...])

    @pl.when(last_step())
    def _():
        rounded = summed[...].T.astype(BF16)
        features[...] = rounded
        parts = network(rounded, *bf16_weights(first, hidden, feature, density))
        colors = parts[6]
        reach, kept, passing = transmittance(parts[8], samples)
        rows = passing.shape[0]
        value = jnp.zeros_like(passing)
        for s in range(samples):
            value = value + reach[s] * (1.0 - kept[s]) * colors[s * rows : (s + 1) * rows]
        message[:, :WIDTH] = value
        message[:, WIDTH:] = passing


def forward_rays_kernel(count, rows, ray_count, segs, samples, lines, *refs):
    local_in, owner_in = refs[:6], refs[6:9]
    features, ray_out, received = refs[9:12]
    message, factor, table, summed = refs[12:16]

    @pl.when(first_step())
    def _():
        enter(count)

    forward_kernel(samples, lines, *local_in, message, features, factor, table, summed)

    @pl.when(last_step())
    def _():
        owner_kernel(
            count, rows, ray_count, segs, message, *owner_in, ray_out, received, *refs[16:], greeted=True
        )


def silu_slope(pre, gate):
    return gate * (1.0 + pre * (1.0 - gate))


def backward_kernel(
    samples,
    lines,
    payload,
    planes,
    first,
    hidden,
    feature,
    density,
    features,
    incoming,
    plane_grad,
    first_grad,
    hidden_grad,
    feature_grad,
    density_grad,
    pose_grad,
    factor,
    slope,
    table,
    cot,
    cot_rows,
    product,
    point_grad,
):
    @pl.when(first_step())
    def _():
        fill_factors(coordinate_rows(payload[...], samples), factor, slope)
        point_grad[...] = jnp.zeros_like(point_grad)
        weight1, weight2, heads = bf16_weights(first, hidden, feature, density)
        pre1, gate1, hidden1, pre2, gate2, hidden2, colors, raw, thick = network(
            features[...], weight1, weight2, heads
        )
        reach, kept, passing = transmittance(thick, samples)
        rows = passing.shape[0]
        feature_cot = incoming[:, :WIDTH]
        pass_cot = incoming[:, WIDTH:] * passing
        behind = pass_cot
        color_cots = [None] * samples
        depth_cots = [None] * samples
        for s in reversed(range(samples)):
            here = colors[s * rows : (s + 1) * rows]
            along = jnp.sum(feature_cot * here, axis=1, keepdims=True)
            weight = reach[s] * (1.0 - kept[s])
            color_cots[s] = weight * feature_cot * (1.0 - here * here)
            depth_cots[s] = along * reach[s] * kept[s] - behind
            behind = behind + along * weight
        raw_cot = jnp.concatenate(depth_cots, axis=0) * STEP * jax.nn.sigmoid(raw)
        lane = lax.broadcasted_iota(jnp.int32, raw_cot.shape, 1)
        raw_cot = jnp.where(lane == 0, raw_cot, 0.0)
        last_cot = jnp.concatenate([jnp.concatenate(color_cots, axis=0), raw_cot], axis=1)
        last_cot = last_cot.astype(BF16)
        feature_grad[0] = dot(hidden2, last_cot[:, :WIDTH], 0, 0).astype(BF16).astype(F32)
        by_density = dot(last_cot[:, WIDTH:], hidden2, 0, 0)
        density_grad[...] = by_density[0:1].astype(BF16).astype(F32)
        cot2 = dot(last_cot, heads, 1, 1).astype(BF16).astype(F32)
        cot2 = (cot2 * silu_slope(pre2, gate2)).astype(BF16)
        hidden_grad[0, 0] = dot(hidden1, cot2, 0, 0).astype(BF16).astype(F32)
        cot1 = dot(cot2, weight2, 1, 1).astype(BF16).astype(F32)
        cot1 = (cot1 * silu_slope(pre1, gate1)).astype(BF16)
        first_grad[0] = dot(features[...], cot1, 0, 0).astype(BF16).astype(F32)
        sample_cot = dot(cot1, weight1, 1, 1)
        cot[...] = sample_cot.astype(BF16)
        cot_rows[...] = sample_cot.T.astype(BF16)

    product[...] = dot(planes[0].astype(BF16), cot_rows[...])
    fill_table(factor, table, lines)
    plane_grad[0] = dot(table[...], cot[...])
    row_axis, col_axis, first_line = block_place(lines)

    def one(chunk, carry):
        lanes = pl.ds(pl.multiple_of(chunk * WIDTH, WIDTH), WIDTH)
        col, col_slope = factor[col_axis, :, lanes], slope[col_axis, :, lanes]
        here = pl.ds(pl.multiple_of(first_line, 8), lines)
        rows, row_slopes = factor[row_axis, here, lanes], slope[row_axis, here, lanes]
        row_total = jnp.zeros((8, WIDTH), F32)
        col_total = jnp.zeros((8, WIDTH), F32)
        for line in range(lines):
            piece = product[line * SIDE : (line + 1) * SIDE, lanes]
            by_col = (piece * col).reshape(SIDE // 8, 8, WIDTH).sum(0)
            by_slope = (piece * col_slope).reshape(SIDE // 8, 8, WIDTH).sum(0)
            row_total = row_total + by_col * row_slopes[line : line + 1]
            col_total = col_total + by_slope * rows[line : line + 1]
        point_grad[row_axis, :, lanes] += row_total
        point_grad[col_axis, :, lanes] += col_total
        return carry

    lax.fori_loop(0, cot.shape[0] // WIDTH, one, 0, unroll=True)

    @pl.when(last_step())
    def _():
        columns = payload[...].T
        rows = columns.shape[1]
        base = 3 * samples
        anchor = [columns[base + c : base + c + 1] for c in range(3)]
        direction = [columns[base + 3 + c : base + 4 + c] for c in range(3)]
        place_grad, way_grad = [], []
        for c in range(3):
            whole = jnp.sum(point_grad[c], axis=0, keepdims=True)
            place = jnp.zeros((1, rows), F32)
            way = jnp.zeros((1, rows), F32)
            for s in range(samples):
                piece = whole[:, s * rows : (s + 1) * rows]
                place = place + piece
                way = way + piece * columns[base + 6 + s : base + 7 + s]
            place_grad.append(place)
            way_grad.append(way)
        turn = []
        for c in range(3):
            d, e = (c + 1) % 3, (c + 2) % 3
            turn.append(
                anchor[d] * place_grad[e]
                - anchor[e] * place_grad[d]
                + direction[d] * way_grad[e]
                - direction[e] * way_grad[d]
            )
        stacked = jnp.concatenate(turn + place_grad + [jnp.zeros((2, rows), F32)], axis=0)
        camera = payload[:, base + 6 + samples : base + 7 + samples]
        cameras = pose_grad.shape[1]
        named = lax.broadcasted_iota(jnp.int32, (rows, cameras), 1).astype(F32) == camera
        pose_grad[...] = exact_dot(stacked, named.astype(F32))


def whole_spec(shape):
    return pl.BlockSpec(shape, lambda *place: (0,) * len(shape))


def shaped(*shape):
    return jax.ShapeDtypeStruct(shape, F32)


def remote_params(number):
    return pltpu.CompilerParams(
        collective_id=number, has_side_effects=True, vmem_limit_bytes=VMEM_BYTES
    )


def per_device(
    anchors,
    directions,
    ray_start,
    camera_ids,
    brick_ids,
    brick_rank,
    targets,
    planes,
    first_weight,
    hidden_weight,
    feature_weight,
    density_weight,
    poses,
):
    count = lax.axis_size(AXES)
    ray_count, segs = brick_ids.shape
    samples = 4
    cap = 2 * ray_count * segs // count
    rows = -(-cap // 8) * 8
    listed = ray_count * segs
    slots = count * cap
    total = slots * samples
    cameras = poses.shape[1]
    in_vmem = pl.BlockSpec(memory_space=pltpu.VMEM)

    per_ray = jnp.concatenate(
        [anchors, directions, ray_start[None], camera_ids.astype(F32)[None]], axis=0
    )
    listing = jnp.concatenate(
        [
            jnp.tile(per_ray, (1, segs)),
            brick_rank.T.reshape(1, listed).astype(F32),
            brick_ids.T.reshape(1, listed).astype(F32),
        ],
        axis=0,
    )

    def narrow(padded):
        if rows == cap:
            return padded
        return padded.reshape(count, rows, -1)[:, :cap].reshape(slots, -1)

    def widen(packed):
        if rows == cap:
            return packed
        grouped = packed.reshape(count, cap, -1)
        return jnp.pad(grouped, ((0, 0), (0, rows - cap), (0, 0))).reshape(count * rows, -1)

    pair = [pltpu.SemaphoreType.DMA((count,)), pltpu.SemaphoreType.DMA((count,))]
    received, route = pl.pallas_call(
        functools.partial(points_kernel, count, rows, samples),
        out_shape=[shaped(count * rows, WIDTH), shaped(count * rows, listed)],
        in_specs=[in_vmem] * 2,
        out_specs=[in_vmem] * 2,
        scratch_shapes=[pltpu.VMEM((count * rows, WIDTH), F32)] * 2 + pair,
        compiler_params=remote_params(0),
        name="send_points",
    )(listing, poses)
    received = narrow(received)

    weights = (first_weight, hidden_weight, feature_weight, density_weight)
    channels = planes.shape[2]
    lines = 16
    cells = lines * SIDE
    grid = (3, SIDE // lines)
    plane_spec = pl.BlockSpec((1, cells, channels), lambda q, i: (0, q * (SIDE // lines) + i, 0))
    local = pltpu.CompilerParams(vmem_limit_bytes=VMEM_BYTES)
    wide = (count * rows, 2 * WIDTH)
    lookup_scratch = [
        pltpu.VMEM((3, SIDE, total), F32),
        pltpu.VMEM((cells, total), BF16),
        pltpu.VMEM((channels, total), F32),
    ]
    if rows == cap:
        owner_in = (route, listing, targets)
        features, ray_feature, incoming = pl.pallas_call(
            functools.partial(forward_rays_kernel, count, rows, ray_count, segs, samples, lines),
            grid=grid,
            out_shape=[
                jax.ShapeDtypeStruct((total, channels), BF16),
                shaped(ray_count, WIDTH),
                shaped(*wide),
            ],
            in_specs=[whole_spec(received.shape), plane_spec]
            + [whole_spec(w.shape) for w in weights + owner_in],
            out_specs=[
                whole_spec((total, channels)),
                whole_spec((ray_count, WIDTH)),
                whole_spec(wide),
            ],
            scratch_shapes=[pltpu.VMEM(wide, F32)]
            + lookup_scratch
            + [pltpu.VMEM(wide, F32)] * 3
            + pair
            + pair,
            compiler_params=remote_params(1),
            name="brick_forward_rays",
        )(received, planes, *weights, *owner_in)
    else:
        message, features = pl.pallas_call(
            functools.partial(forward_kernel, samples, lines),
            grid=grid,
            out_shape=[shaped(slots, 2 * WIDTH), jax.ShapeDtypeStruct((total, channels), BF16)],
            in_specs=[whole_spec(received.shape), plane_spec]
            + [whole_spec(w.shape) for w in weights],
            out_specs=[whole_spec((slots, 2 * WIDTH)), whole_spec((total, channels))],
            scratch_shapes=[
                pltpu.VMEM((3, SIDE, total), F32),
                pltpu.VMEM((cells, total), BF16),
                pltpu.VMEM((channels, total), F32),
            ],
            compiler_params=local,
            name="brick_forward",
        )(received, planes, *weights)

        ray_feature, incoming = pl.pallas_call(
            functools.partial(owner_kernel, count, rows, ray_count, segs),
            out_shape=[shaped(ray_count, WIDTH), shaped(*wide)],
            in_specs=[in_vmem] * 4,
            out_specs=[in_vmem] * 2,
            scratch_shapes=[pltpu.VMEM(wide, F32)] * 3 + pair + pair,
            compiler_params=remote_params(1),
            name="rays",
        )(widen(message), route, listing, targets)
    incoming = narrow(incoming)

    plane_grad, *weight_grads, pose_local = pl.pallas_call(
        functools.partial(backward_kernel, samples, lines),
        grid=grid,
        out_shape=[
            shaped(*planes.shape),
            *(shaped(*w.shape) for w in weights),
            shaped(8, cameras),
        ],
        in_specs=[whole_spec(received.shape), plane_spec]
        + [whole_spec(w.shape) for w in weights + (features, incoming)],
        out_specs=[plane_spec]
        + [whole_spec(w.shape) for w in weights]
        + [whole_spec((8, cameras))],
        scratch_shapes=[
            pltpu.VMEM((3, SIDE, total), F32),
            pltpu.VMEM((3, SIDE, total), F32),
            pltpu.VMEM((cells, total), BF16),
            pltpu.VMEM((total, channels), BF16),
            pltpu.VMEM((channels, total), BF16),
            pltpu.VMEM((cells, total), F32),
            pltpu.VMEM((3, 8, total), F32),
        ],
        compiler_params=local,
        name="brick_backward",
    )(received, planes, *weights, features, incoming)

    far, near = (lax.axis_size(axis) for axis in AXES)
    pose_grad = pl.pallas_call(
        functools.partial(pose_kernel, 8),
        out_shape=shaped(*poses.shape),
        in_specs=[in_vmem],
        out_specs=in_vmem,
        scratch_shapes=[
            pltpu.VMEM((8 * near, cameras), F32),
            pltpu.VMEM((8, cameras), F32),
            pltpu.VMEM((8 * far, cameras), F32),
        ]
        + [pltpu.SemaphoreType.DMA((near,))] * 2
        + [pltpu.SemaphoreType.DMA((far,))] * 2,
        compiler_params=remote_params(2),
        name="sum_poses",
    )(pose_local)
    return (ray_feature, plane_grad, *weight_grads, pose_grad)


def solution(mesh):
    split = P(AXES)
    in_specs = (P(None, AXES), P(None, AXES)) + (split,) * 10 + (P(),)
    out_specs = (split,) * 6 + (P(),)
    return jax.shard_map(
        per_device, mesh=mesh, in_specs=in_specs, out_specs=out_specs, check_vma=False
    )
```
